256 devices in a mesh: gx: 8 (over x, core), gy: 16 (over z_hi, y), gz: 2 (over z_lo).
Axes of the slice: x: 4, y: 4, z: 8 (z_hi: 4, z_lo: 2; z = z_hi * 2 + z_lo), core: 2. Of those that a mesh axis runs over, the one named last changes fastest.
Arguments:
- kelvin_before_scan: float32 [128, 512, 256], P('gx', 'gy', 'gz'), may hold values from -5 to 5
- conductance_coefficient: float32 [128, 512, 256], P('gx', 'gy', 'gz'), may hold values from 0.8 to 1
- remelted_flag: int32 [128, 512, 256], P('gx', 'gy', 'gz'), may hold values 0 or 1
- germ_site_flag: int32 [128, 512, 256], P('gx', ('gy', 'gz')), may hold values 0 or 1
- nucleus_grain_label: int32 [128, 512, 256], P('gx', ('gy', 'gz')), may hold values from 1 to 8192
- lattice_pose_number: int32 [128, 512, 256], P('gx', ('gy', 'gz')), may hold values from 0 to 63
- engulf_outcome: int32 [2, 128, 512, 256], P(None, 'gx', ('gy', 'gz')), may hold values from 0 to 6, as said below
- expanding_patch_roster: int32 [8, 32, 8], P('gx', ('gy', 'gz')), may hold values from -1 to 7, as said below
- lattice_pose_turns: float32 [3, 64], replicated, may hold values from -3.140625 to 3.140625
Outputs:
- temperature_out: float32 [128, 512, 256], P('gx', 'gy', 'gz')
- envelope: float32 [128, 512, 256], P('gx', ('gy', 'gz'))
- grain_map: int32 [128, 512, 256], P('gx', ('gy', 'gz'))
The draws below stay inside these ranges and needn't reach their ends.
Inputs may be any that keep to these rules, and one draw needn't show every extreme that they name: `engulf_outcome`: 0 means no capture in that step; 1 to 6 name the capturing neighbour: -x, +x, -y, +y, -z, +z in that order. `expanding_patch_roster`: each device's row starts with 1 to 8 distinct tile numbers of 0 to 7 and is filled up with -1; some device lists all 8 tiles.
All inputs are finite; a program needn't handle non-finite values. No bound on the sum of `remelted_flag` or of `germ_site_flag` on one device may be relied on, other than what follows from the above.
Results may differ from the reference program's by a relative error of at most 0.0004.
Values sent between devices are 32-bit elements; how exact they have to be, the bound alone decides.
A program may use at most 64 MiB of HBM per device.

```python
import math
import jax
import jax.numpy as jnp

SUBSTEPS = 6
NORI = 64
GRAINS = 8192
TILES = 8
COUNT_LEADING = 128
COUNT_MIDDLE = 512
COUNT_TRAILING = 256
N_GX = 8
N_GY = 16
N_GZ = 2


def draw_kelvin_before_scan(key, part):
    key = jax.random.fold_in(key, 11)
    shape = (COUNT_LEADING, COUNT_MIDDLE, COUNT_TRAILING)
    values = jax.random.truncated_normal(key, -5.0, 5.0, shape, jnp.float32)
    return jnp.clip(values, -5.0, 5.0).astype(jnp.float32)


def draw_engulf_outcome(key, part):
    outcome = jax.random.randint(key, (2, COUNT_LEADING, COUNT_MIDDLE, COUNT_TRAILING), 0, 24, dtype=jnp.int32)
    return jnp.where(outcome < 6, outcome + 1, 0).astype(jnp.int32)


def draw_expanding_patch_roster(key, part):
    groups = N_GX * N_GY * N_GZ
    rarely = jax.random.randint(jax.random.fold_in(key, 1), (groups,), 0, 8, dtype=jnp.int32)
    smaller = jax.random.randint(jax.random.fold_in(key, 2), (groups,), 1, 3, dtype=jnp.int32)
    counts = jnp.where(rarely == 0, TILES, smaller)
    full_at = jax.random.randint(jax.random.fold_in(key, 3), (), 0, groups, dtype=jnp.int32)
    counts = jnp.where(jnp.arange(groups, dtype=jnp.int32) == full_at, TILES, counts)
    group_keys = jax.random.split(jax.random.fold_in(key, 4), groups)

    def shuffle_one(one_key):
        return jax.random.permutation(one_key, TILES).astype(jnp.int32)
    orders = jax.vmap(shuffle_one)(group_keys)
    listed = jnp.where(jnp.arange(TILES, dtype=jnp.int32)[None, :] < counts[:, None], orders, -1)
    return listed.reshape(N_GX, N_GY * N_GZ, TILES).astype(jnp.int32)


def place_ends(result, own_key, least, high):
    longest = result.shape.index(max(result.shape))
    spots = []
    for shift in (0, 1):
        where = [jax.random.randint(jax.random.fold_in(own_key, axis), (), 0, length) for axis, length in enumerate(result.shape)]
        where[longest] = (where[longest] + shift) % result.shape[longest]
        spots.append(tuple(where))
    return result.at[spots[0]].set(least).at[spots[1]].set(high)


def block_scale(own_key, extent, shards, smallest, largest):
    loudness = 1.0
    for axis_at, parts in shards:
        heights = jax.random.uniform(jax.random.fold_in(jax.random.fold_in(own_key, 6), axis_at), (parts,), jnp.float32, smallest / len(shards), largest / len(shards))
        loudness = loudness * jnp.repeat(jnp.exp(heights), extent[axis_at] // parts).reshape((-1,) + (1,) * (len(extent) - 1 - axis_at))
    return loudness


def setup_inputs(seed: int = 0) -> dict:
    arg_keys = jax.random.split(jax.random.key(seed), 10)
    kelvin_before_scan = draw_kelvin_before_scan(jax.random.fold_in(arg_keys[9], 71), 0)
    conductance_coefficient = jnp.clip(jnp.exp(math.log(1.0) - 0.22314354 * jax.random.uniform(arg_keys[1], (COUNT_LEADING, COUNT_MIDDLE, COUNT_TRAILING), jnp.float32) ** block_scale(arg_keys[1], (COUNT_LEADING, COUNT_MIDDLE, COUNT_TRAILING), ((0, 8), (1, 16), (2, 2)), -0.2, 0.2)), 0.8, 1.0)
    remelted_flag = place_ends((jax.random.randint(arg_keys[2], (COUNT_LEADING, COUNT_MIDDLE, COUNT_TRAILING), 0, 20) < 19).astype(jnp.int32), jax.random.fold_in(arg_keys[2], 1), 0, 1)
    germ_site_flag = place_ends((jax.random.randint(arg_keys[3], (COUNT_LEADING, COUNT_MIDDLE, COUNT_TRAILING), 0, 5) < 2).astype(jnp.int32), jax.random.fold_in(arg_keys[3], 1), 0, 1)
    nucleus_grain_label = place_ends(jax.random.randint(arg_keys[4], (COUNT_LEADING, COUNT_MIDDLE, COUNT_TRAILING), 1, GRAINS + 1), jax.random.fold_in(arg_keys[4], 1), 1, GRAINS).astype(jnp.int32)
    lattice_pose_number = place_ends(jax.random.randint(arg_keys[5], (COUNT_LEADING, COUNT_MIDDLE, COUNT_TRAILING), 0, NORI), jax.random.fold_in(arg_keys[5], 1), 0, NORI - 1).astype(jnp.int32)
    engulf_outcome = draw_engulf_outcome(jax.random.fold_in(arg_keys[9], 71), 0)
    expanding_patch_roster = draw_expanding_patch_roster(jax.random.fold_in(arg_keys[9], 71), 0)
    lattice_pose_turns = jnp.clip(jax.random.uniform(arg_keys[8], (3, NORI), jnp.float32, -3.140625, 3.140625), -3.140625, 3.140625)
    return {"kelvin_before_scan": kelvin_before_scan, "conductance_coefficient": conductance_coefficient, "remelted_flag": remelted_flag, "germ_site_flag": germ_site_flag, "nucleus_grain_label": nucleus_grain_label, "lattice_pose_number": lattice_pose_number, "engulf_outcome": engulf_outcome, "expanding_patch_roster": expanding_patch_roster, "lattice_pose_turns": lattice_pose_turns}


FREEZE_RELEASE = 2.0
LIQUID_BOOST = 0.5
TIME_STEP = 0.1
SCAN_LINE_INPUT = 1.5
POWDER_SHARE = 0.25
GROWTH_COEF = 1.0


def melting_point(stored_caloric_content):
    return jnp.where(stored_caloric_content < 0.0, stored_caloric_content,
                     jnp.where(stored_caloric_content > 1.0 + FREEZE_RELEASE, stored_caloric_content - FREEZE_RELEASE, stored_caloric_content / (1.0 + FREEZE_RELEASE)))


def face_flux(center_t, center_k, other_t, other_k):
    denominator = center_k + other_k
    safe_denom = jnp.where(denominator > 0.0, denominator, 1.0)
    return 2.0 * center_k * other_k / safe_denom * (other_t - center_t)


def heat_substep(padded_heat, cond_pad):
    current_fields = melting_point(padded_heat)
    conducts = cond_pad * (1.0 + LIQUID_BOOST * jnp.clip(current_fields, 0.0, 1.0))
    center_t = current_fields[1:-1, 1:-1, 1:-1]
    center_k = conducts[1:-1, 1:-1, 1:-1]
    shifts = ((slice(None, -2), slice(1, -1), slice(1, -1)),
              (slice(2, None), slice(1, -1), slice(1, -1)),
              (slice(1, -1), slice(None, -2), slice(1, -1)),
              (slice(1, -1), slice(2, None), slice(1, -1)),
              (slice(1, -1), slice(1, -1), slice(None, -2)),
              (slice(1, -1), slice(1, -1), slice(2, None)))
    flux_total = jnp.zeros_like(center_t)
    for window in shifts:
        flux_total = flux_total + face_flux(center_t, center_k, current_fields[window], conducts[window])
    return padded_heat[1:-1, 1:-1, 1:-1] + TIME_STEP * flux_total


def envelope_reach(angles):
    cos_a, sin_a = jnp.cos(angles[0]), jnp.sin(angles[0])
    cos_b, sin_b = jnp.cos(angles[1]), jnp.sin(angles[1])
    cos_c, sin_c = jnp.cos(angles[2]), jnp.sin(angles[2])
    row_x = jnp.abs(cos_a * cos_c - sin_a * sin_c * cos_b) + jnp.abs(-cos_a * sin_c - sin_a * cos_c * cos_b) + jnp.abs(sin_a * sin_b)
    row_y = jnp.abs(sin_a * cos_c + cos_a * sin_c * cos_b) + jnp.abs(-sin_a * sin_c + cos_a * cos_c * cos_b) + jnp.abs(-cos_a * sin_b)
    row_z = jnp.abs(sin_c * sin_b) + jnp.abs(cos_c * sin_b) + jnp.abs(cos_b)
    return jnp.stack([row_x, row_y, row_z])


def growth_speed(cooling, liquid_time):
    undercool = jnp.maximum(cooling, 0.0) * (0.5 + liquid_time)
    return GROWTH_COEF * undercool * undercool


def neighbour_pick(padded, capture_code):
    views = (padded[:-2, 1:-1, 1:-1], padded[2:, 1:-1, 1:-1],
             padded[1:-1, :-2, 1:-1], padded[1:-1, 2:, 1:-1],
             padded[1:-1, 1:-1, :-2], padded[1:-1, 1:-1, 2:])
    picked = jnp.zeros_like(views[0])
    for number, window_view in enumerate(views):
        picked = jnp.where(capture_code == number + 1, window_view, picked)
    return picked


def reference(kelvin_before_scan, conductance_coefficient, remelted_flag, germ_site_flag, nucleus_grain_label, lattice_pose_number, engulf_outcome, expanding_patch_roster, lattice_pose_turns):
    molten_proportion = remelted_flag.astype(jnp.float32)
    base_cond = conductance_coefficient * (POWDER_SHARE + (1.0 - POWDER_SHARE) * molten_proportion)
    opening_kelvin_level = kelvin_before_scan + SCAN_LINE_INPUT * molten_proportion
    stored_caloric_content = opening_kelvin_level + FREEZE_RELEASE * jnp.clip(opening_kelvin_level, 0.0, 1.0)
    cond_pad = jnp.pad(base_cond, 1)
    liquid_sum = jnp.zeros_like(stored_caloric_content)
    previous = stored_caloric_content
    current_fields = stored_caloric_content
    for step_index in range(SUBSTEPS):
        stored_caloric_content = heat_substep(jnp.pad(stored_caloric_content, 1), cond_pad)
        previous = current_fields
        current_fields = melting_point(stored_caloric_content)
        liquid_sum = liquid_sum + jnp.clip(current_fields, 0.0, 1.0)
    liquid_time = TIME_STEP * liquid_sum
    cooling = (previous - current_fields) / TIME_STEP
    speed = growth_speed(cooling, liquid_time)

    table_size = lattice_pose_turns.shape[1]
    reach = envelope_reach(lattice_pose_turns)
    label = germ_site_flag * (nucleus_grain_label * table_size + lattice_pose_number)
    envelope = jnp.zeros(speed.shape, jnp.float32)
    gx_count, group_count, tile_count = expanding_patch_roster.shape
    tile_ids = jnp.arange(tile_count, dtype=jnp.int32)
    listed_on = jnp.any(expanding_patch_roster[:, :, :, None] == tile_ids[None, None, None, :], axis=2)
    full_x, full_y = speed.shape[0], speed.shape[1]
    rows_tile = full_x // (gx_count * tile_count)
    cols_dev = full_y // group_count
    cell_on = jnp.broadcast_to(jnp.transpose(listed_on, (0, 2, 1))[:, :, None, :, None],
                               (gx_count, tile_count, rows_tile, group_count, cols_dev)).reshape(full_x, full_y)
    active = cell_on[:, :, None]
    for growth_index in range(2):
        capture_code = engulf_outcome[growth_index]
        grown = envelope + jnp.where(label > 0, speed, 0.0)
        side_grown = neighbour_pick(jnp.pad(grown, 1), capture_code)
        side_label = neighbour_pick(jnp.pad(label, 1), capture_code)
        axis_code = (capture_code - 1) // 2
        side_reach = reach[axis_code, side_label % table_size]
        captured = jnp.maximum(side_grown - side_reach, 0.0)
        taken = capture_code > 0
        new_envelope = jnp.where(taken, captured, grown)
        new_label = jnp.where(taken, side_label, label)
        envelope = jnp.where(active, new_envelope, envelope)
        label = jnp.where(active, new_label, label)
    return current_fields, envelope, label // table_size
```

```python
import functools

import jax
import jax.numpy as jnp
from jax import lax
from jax.experimental import pallas as pl
from jax.experimental.pallas import tpu as pltpu
from jax.sharding import PartitionSpec as P

MESH = pl.DeviceIdType.MESH
D = 6
NX, NY, NZ = 16, 32, 128
EX = NX + 2 * D
OY = 8
EY = NY + 2 * OY
PITCH = 3 * D
GR = 16
GX = NX + 4
GY = GR + 16
TINY = 1e-30


def lanes(shape):
    return lax.broadcasted_iota(jnp.int32, shape, 1)


def rows(shape):
    return lax.broadcasted_iota(jnp.int32, shape, 0)


def clip03(heat):
    return jnp.minimum(jnp.maximum(heat, 0.0), 3.0)


def state(heat, base):
    solid = clip03(heat)
    return heat - solid * (2.0 / 3.0), base * (1.0 + solid * (1.0 / 6.0))


def face(temp, cond, temp_next, cond_next):
    total = jnp.maximum(cond + cond_next, TINY)
    return (cond * cond_next) * pltpu.reciprocal(total, approx=True) * (temp_next - temp)


def roll(value, amount, axis):
    return pltpu.roll(value, amount % value.shape[axis], axis)


class Main:
    def __init__(self):
        self.lane_end = lanes((EY, NZ)) == NZ - 1

    def up(self, v):
        return roll(v, -1, 0)

    def down(self, v):
        return roll(v, 1, 0)

    def edge(self, flux):
        return jnp.where(self.lane_end, 0.0, flux)


class Strip:
    def __init__(self):
        self.first = rows((8, NZ)) == 0
        self.last = rows((8, NZ)) == 7

    def up(self, v):
        turned = roll(v, -1, 0)
        return jnp.where(self.last, roll(turned, -PITCH, 1), turned)

    def down(self, v):
        turned = roll(v, 1, 0)
        return jnp.where(self.first, roll(turned, PITCH, 1), turned)

    def edge(self, flux):
        return flux


def substep(src, dst, base, step, form, finish=None):
    first, stop = step, EX - step
    before_t, before_k = state(src[first - 1], base[first - 1])
    here_t, here_k = state(src[first], base[first])
    into = face(before_t, before_k, here_t, here_k)

    def slab(x, carry):
        here_t, here_k, into = carry
        next_t, next_k = state(src[x + 1], base[x + 1])
        out_of = face(here_t, here_k, next_t, next_k)
        along_y = face(here_t, here_k, form.up(here_t), form.up(here_k))
        along_z = form.edge(face(here_t, here_k, roll(here_t, -1, 1), roll(here_k, -1, 1)))
        total = (out_of - into) + (along_y - form.down(along_y)) + (along_z - roll(along_z, 1, 1))
        heat = src[x] + 0.2 * total
        if finish is None:
            dst[x] = heat
        else:
            finish(x, here_t, heat)
        return next_t, next_k, out_of

    def pair(i, carry):
        x = first + 2 * i
        return slab(x + 1, slab(x, carry))

    lax.fori_loop(0, (stop - first) // 2, pair, (here_t, here_k, into))


def outcome(history, x, temp_before, heat):
    solid = clip03(heat)
    temp = heat - solid * (2.0 / 3.0)
    liquid = solid
    for s in range(1, 6):
        liquid = liquid + clip03(history[s, x])
    cooling = (temp_before - temp) * 10.0
    under = jnp.maximum(cooling, 0.0) * (0.5 + liquid * (0.1 / 3.0))
    return temp, under * under


def shift_z(low, high):
    lane = lanes(low.shape)
    low_down, high_down = roll(low, 1, 1), roll(high, 1, 1)
    low_up, high_up = roll(low, -1, 1), roll(high, -1, 1)
    zero = jnp.zeros_like(low)
    down = (jnp.where(lane == 0, zero, low_down), jnp.where(lane == 0, low_down, high_down))
    up = (jnp.where(lane == NZ - 1, high_up, low_up), jnp.where(lane == NZ - 1, zero, high_up))
    return down, up


def pick(ref, x, codes):
    here = (ref[0, x], ref[1, x])
    down, up = shift_z(*here)
    picked = []
    for half in range(2):
        code = codes[half]
        views = (
            ref[half, x - 1],
            ref[half, x + 1],
            roll(here[half], 1, 0),
            roll(here[half], -1, 0),
            down[half],
            up[half],
        )
        value = jnp.zeros_like(here[half])
        for number, view in enumerate(views):
            value = jnp.where(code == number + 1, view, value)
        picked.append(value)
    return picked


def reach_rows(turns):
    cos_a, sin_a = jnp.cos(turns[0:1]), jnp.sin(turns[0:1])
    cos_b, sin_b = jnp.cos(turns[1:2]), jnp.sin(turns[1:2])
    cos_c, sin_c = jnp.cos(turns[2:3]), jnp.sin(turns[2:3])
    row_x = (
        jnp.abs(cos_a * cos_c - sin_a * sin_c * cos_b)
        + jnp.abs(-cos_a * sin_c - sin_a * cos_c * cos_b)
        + jnp.abs(sin_a * sin_b)
    )
    row_y = (
        jnp.abs(sin_a * cos_c + cos_a * sin_c * cos_b)
        + jnp.abs(-sin_a * sin_c + cos_a * cos_c * cos_b)
        + jnp.abs(-cos_a * sin_b)
    )
    row_z = jnp.abs(sin_c * sin_b) + jnp.abs(cos_c * sin_b) + jnp.abs(cos_b)
    return row_x, row_y, row_z


def lookup(tables, side, code):
    pose = side & 63
    axis = jnp.maximum(code - 1, 0) >> 1
    parts = []
    for tile in range(side.shape[0] // 8):
        cut = slice(8 * tile, 8 * tile + 8)
        index = pose[cut] + ((axis[cut] & 1) << 6)
        xy = jnp.take_along_axis(tables[0], index, axis=1, mode="promise_in_bounds")
        z = jnp.take_along_axis(tables[1], index, axis=1, mode="promise_in_bounds")
        parts.append(jnp.where(axis[cut] == 2, z, xy))
    return jnp.concatenate(parts, axis=0)


def kernel(
    kelvin, conductance, melted, germ, nucleus, pose, captured, roster, turns,
    temp_out, env_out, grain_out,
    bricks, history, strip_h, strip_b, strip_out, strip_in, speed,
    strip_t, strip_s, lab, lab1, reach1, reach2, gspeed, grown, grown1, env1,
    heat_send, heat_recv, strip_send, strip_recv,
    speed_send, speed_recv_a, speed_recv_b, local_sem, lab_send, lab_recv,
):
    gx, gy, gz = (lax.axis_index(a) for a in ("gx", "gy", "gz"))
    ngx, ngy = lax.axis_size("gx"), lax.axis_size("gy")

    def at(dx, dy, z):
        return (lax.rem(gx + dx + ngx, ngx), lax.rem(gy + dy + ngy, ngy), z)

    other = 1 - gz
    cross = 2 * gz - 1
    xy = [(dx, dy) for dx in (-1, 0, 1) for dy in (-1, 0, 1) if (dx, dy) != (0, 0)]
    greeted = [at(dx, dy, gz) for dx, dy in xy]
    greeted += [at(dx, 0, other) for dx in (-1, 0, 1)]
    greeted += [at(dx, cross, other) for dx in (-1, 0, 1)]
    barrier = pltpu.get_barrier_semaphore()
    for device in greeted:
        pl.semaphore_signal(barrier, inc=1, device_id=device, device_id_type=MESH)

    def send(src, dst, send_sem, recv_sem, device):
        copy = pltpu.make_async_remote_copy(
            src_ref=src, dst_ref=dst, send_sem=send_sem, recv_sem=recv_sem,
            device_id=device, device_id_type=MESH,
        )
        copy.start()
        return copy

    own_rows = pl.ds(OY, NY)

    def opening(x, _):
        melt = melted[x].astype(jnp.float32)
        start = kelvin[x] + 1.5 * melt
        bricks[0, D + x, own_rows] = start + 2.0 * jnp.clip(start, 0.0, 1.0)
        bricks[1, D + x, own_rows] = conductance[x] * (0.25 + 0.75 * melt)
        return 0

    lax.fori_loop(0, NX, opening, 0)

    tiles = [roster[0, 0, i] for i in range(8)]

    def seeds(x, _):
        tile = x // 2
        active = tiles[0] == tile
        for number in tiles[1:]:
            active = jnp.logical_or(active, number == tile)
        for half in range(2):
            cut = pl.ds(half * NZ, NZ)
            label = germ[x, :, cut] * (nucleus[x, :, cut] * 64 + pose[x, :, cut])
            lab[0, half, 2 + x, pl.ds(8, GR)] = label
            for g in range(2):
                lab[1 + g, half, 2 + x, pl.ds(8, GR)] = jnp.where(
                    active, captured[g, x, :, cut], -1
                )
        return 0

    lax.fori_loop(0, NX, seeds, 0)

    pl.semaphore_wait(barrier, len(greeted))

    copies = []
    for i, (dx, dy) in enumerate(xy):
        deep = D if dx == 0 or dy == 0 else D - 1
        src_x = {-1: (D, deep), 0: (D, NX), 1: (D + NX - deep, deep)}[dx]
        dst_x = {-1: D + NX, 0: D, 1: D - deep}[dx]
        src_y = {-1: (OY, deep), 0: (OY, NY), 1: (OY + NY - deep, deep)}[dy]
        dst_y = {-1: OY + NY, 0: OY, 1: OY - deep}[dy]
        copies.append(send(
            bricks.at[:, pl.ds(*src_x), pl.ds(*src_y)],
            bricks.at[:, pl.ds(dst_x, src_x[1]), pl.ds(dst_y, src_y[1])],
            heat_send.at[i], heat_recv.at[i], at(dx, dy, gz),
        ))

    lab_copies = []
    for i, (dx, dg) in enumerate(xy):
        deep = 2 if dx == 0 or dg == 0 else 1
        src_x = {-1: (2, deep), 0: (2, NX), 1: (2 + NX - deep, deep)}[dx]
        dst_x = {-1: 2 + NX, 0: 2, 1: 2 - deep}[dx]
        src_y = {-1: (8, deep), 0: (8, GR), 1: (8 + GR - deep, deep)}[dg]
        dst_y = {-1: 8 + GR, 0: 8, 1: 8 - deep}[dg]
        if dg == 0:
            device = at(dx, 0, gz)
        elif dg == 1:
            device = at(dx, gz, other)
        else:
            device = at(dx, gz - 1, other)
        lab_copies.append(send(
            lab.at[pl.ds(0, 2), :, pl.ds(*src_x), pl.ds(*src_y)],
            lab.at[pl.ds(0, 2), :, pl.ds(dst_x, src_x[1]), pl.ds(dst_y, src_y[1])],
            lab_send.at[i], lab_recv.at[i], device,
        ))

    row_x, row_y, row_z = reach_rows(turns[...])
    tables = [
        jnp.broadcast_to(jnp.concatenate(pair, axis=1), (8, NZ))
        for pair in ((row_x, row_y), (row_z, row_z))
    ]

    for copy in copies:
        copy.wait()

    lane8 = lanes((8, NZ))
    row_all = rows((EY, NZ))
    outside_y = ((row_all < OY) & (gy == 0)) | ((row_all >= OY + NY) & (gy == ngy - 1))
    slot = lane8
    for tile in range(1, EY // 8):
        slot = jnp.where(lane8 >= tile * PITCH, lane8 - tile * PITCH, slot)
    in_use = lane8 < PITCH * (EY // 8)
    own_slot = (slot >= D * gz) & (slot < D * gz + 2 * D)
    halo_slot = jnp.logical_not(own_slot) & in_use
    turn = D * (1 - 2 * gz)

    def pack(x, _):
        outside_x = ((x < D) & (gx == 0)) | ((x >= D + NX) & (gx == ngx - 1))
        base = jnp.where(outside_x | outside_y, 0.0, bricks[1, x])
        bricks[1, x] = base
        heat = bricks[0, x]
        history[0, x] = heat
        packed = []
        for value in (heat, base):
            strip = jnp.zeros((8, NZ), jnp.float32)
            for tile in range(EY // 8):
                moved = pltpu.roll(
                    value[8 * tile : 8 * tile + 8], (PITCH * tile + 2 * D - D * gz) % NZ, 1
                )
                mine = own_slot & (lane8 >= tile * PITCH) & (lane8 < (tile + 1) * PITCH)
                strip = jnp.where(mine, moved, strip)
            packed.append(strip)
        strip_h[0, x] = packed[0]
        strip_b[x] = packed[1]
        strip_out[x] = jnp.where(halo_slot, pltpu.roll(packed[1], (turn + NZ) % NZ, 1), packed[0])
        return 0

    lax.fori_loop(0, EX, pack, 0)
    strip_copy = send(
        strip_out, strip_in, strip_send, strip_recv, at(0, 0, other)
    )

    main = Main()
    for step in range(1, 6):
        substep(
            history.at[step - 1], history.at[step], bricks.at[1], step, main
        )

    strip_copy.wait()

    def unpack(x, _):
        got = strip_in[x]
        strip_h[0, x] = jnp.where(halo_slot, pltpu.roll(got, (turn + NZ) % NZ, 1), strip_h[0, x])
        strip_b[x] = jnp.where(halo_slot, pltpu.roll(got, (2 * turn + NZ) % NZ, 1), strip_b[x])
        return 0

    lax.fori_loop(0, EX, unpack, 0)
    form = Strip()
    for step in range(1, 6):
        substep(strip_h.at[step - 1], strip_h.at[step], strip_b, step, form)

    def strip_end(x, temp_before, heat):
        strip_t[x - D], strip_s[x - D] = outcome(strip_h, x, temp_before, heat)

    substep(strip_h.at[5], None, strip_b, 6, form, strip_end)

    near = jnp.where(gz == 0, lane8 - (NZ - D), D - 1 - lane8) >= 0

    def brick_end(x, temp_before, heat):
        temp, fast = outcome(history, x, temp_before, heat)
        for tile in range(NY // 8):
            cut = slice(OY + 8 * tile, OY + 8 * tile + 8)
            back = (NZ - 2 * D + D * gz - PITCH * (tile + 1) + NZ) % NZ
            put = pl.ds(8 * tile, 8)
            temp_out[x - D, put] = jnp.where(
                near, pltpu.roll(strip_t[x - D], back, 1), temp[cut]
            )
            speed[x - D, put] = jnp.where(
                near, pltpu.roll(strip_s[x - D], back, 1), fast[cut]
            )

    substep(history.at[5], None, bricks.at[1], 6, main, brick_end)

    speed_copies = []

    def tell(dx, dy, z, number, recv_sem):
        if dy == 0:
            deep_x = 2
            src_y, dst_y, count_y = 14 * z, 8 - 2 * z, 18
        else:
            deep_x = 1
            count_y = 2 if dx == 0 else 1
            src_y = NY - count_y if dy == 1 else 0
            dst_y = 8 - count_y if dy == 1 else 8 + GR
        src_x = {-1: (0, deep_x), 0: (0, NX), 1: (NX - deep_x, deep_x)}[dx]
        dst_x = {-1: 2 + NX, 0: 2, 1: 2 - deep_x}[dx]
        speed_copies.append(send(
            speed.at[pl.ds(*src_x), pl.ds(src_y, count_y)],
            gspeed.at[gz, pl.ds(dst_x, src_x[1]), pl.ds(dst_y, count_y)],
            speed_send.at[number], recv_sem, at(dx, dy, z),
        ))

    for dx in (-1, 1):
        for z in range(2):
            tell(dx, 0, z, len(speed_copies), speed_recv_a.at[dx + 1, gz])
    for dy, z in ((1, 0), (-1, 1)):
        for dx in (-1, 0, 1):
            tell(dx, dy, z, len(speed_copies), speed_recv_b.at[dx + 1, gz])
    tell(0, 0, other, len(speed_copies), speed_recv_a.at[1, gz])
    keep = pltpu.make_async_copy(
        speed.at[:, pl.ds(14 * gz, 18)],
        gspeed.at[gz, pl.ds(2, NX), pl.ds(8 - 2 * gz, 18)],
        local_sem,
    )
    keep.start()

    for copy in lab_copies:
        copy.wait()
    row_g = rows((GY, NZ))
    outside_g = ((row_g < 8) & (gy + gz == 0)) | (
        (row_g >= 8 + GR) & (gy + gz == ngy)
    )

    def border(x, _):
        outside = outside_g | ((x < 2) & (gx == 0)) | ((x >= 2 + NX) & (gx == ngx - 1))
        for half in range(2):
            lab[0, half, x] = jnp.where(outside, 0, lab[0, half, x])
            lab[1, half, x] = jnp.where(outside, -1, lab[1, half, x])
        return 0

    lax.fori_loop(0, GX, border, 0)

    def first_labels(x, _):
        codes = [lab[1, half, x] for half in range(2)]
        sides = pick(lab.at[0], x, codes)
        for half in range(2):
            lab1[half, x] = jnp.where(codes[half] > 0, sides[half], lab[0, half, x])
            reach1[half, x] = lookup(tables, sides[half], codes[half])
        return 0

    lax.fori_loop(1, GX - 1, first_labels, 0)

    def second_labels(x, _):
        codes = [lab[2, half, x] for half in range(2)]
        sides = pick(lab1, x, codes)
        for half in range(2):
            label = jnp.where(codes[half] > 0, sides[half], lab1[half, x])
            grain_out[x - 2, :, pl.ds(half * NZ, NZ)] = label[8 : 8 + GR] >> 6
            reach2[half, x] = lookup(tables, sides[half], codes[half])
        return 0

    lax.fori_loop(2, GX - 2, second_labels, 0)

    for copy in speed_copies:
        copy.wait_send()
    keep.wait()

    def heard(count_x, count_y, recv_sem):
        pltpu.make_async_remote_copy(
            src_ref=speed.at[pl.ds(0, count_x), pl.ds(0, count_y)],
            dst_ref=gspeed.at[0, pl.ds(0, count_x), pl.ds(0, count_y)],
            send_sem=speed_send.at[0], recv_sem=recv_sem,
            device_id=at(0, 0, other), device_id_type=MESH,
        ).wait_recv()

    for z in range(2):
        for dx in (-1, 1):
            heard(2, 18, speed_recv_a.at[dx + 1, z])
            heard(1, 1, speed_recv_b.at[dx + 1, z])
        heard(NX, 2, speed_recv_b.at[1, z])
    heard(NX, 18, speed_recv_a.at[1, other])

    def seeded(x, _):
        for half in range(2):
            grown[half, x] = jnp.where(lab[0, half, x] > 0, gspeed[half, x], 0.0)
        return 0

    lax.fori_loop(0, GX, seeded, 0)

    def first_growth(x, _):
        codes = [lab[1, half, x] for half in range(2)]
        sides = pick(grown, x, codes)
        for half in range(2):
            code = codes[half]
            caught = jnp.maximum(sides[half] - reach1[half, x], 0.0)
            envelope = jnp.where(
                code > 0, caught, jnp.where(code == 0, grown[half, x], 0.0)
            )
            env1[half, x] = envelope
            grown1[half, x] = envelope + jnp.where(lab1[half, x] > 0, gspeed[half, x], 0.0)
        return 0

    lax.fori_loop(1, GX - 1, first_growth, 0)

    def second_growth(x, _):
        codes = [lab[2, half, x] for half in range(2)]
        sides = pick(grown1, x, codes)
        for half in range(2):
            code = codes[half]
            caught = jnp.maximum(sides[half] - reach2[half, x], 0.0)
            envelope = jnp.where(
                code > 0, caught, jnp.where(code == 0, grown1[half, x], env1[half, x])
            )
            env_out[x - 2, :, pl.ds(half * NZ, NZ)] = envelope[8 : 8 + GR]
        return 0

    lax.fori_loop(2, GX - 2, second_growth, 0)


def body(*args):
    vmem = pl.BlockSpec(memory_space=pltpu.VMEM)
    smem = pl.BlockSpec(memory_space=pltpu.SMEM)
    f32, i32 = jnp.float32, jnp.int32
    dma = pltpu.SemaphoreType.DMA
    growth = (2, GX, GY, NZ)
    return pl.pallas_call(
        kernel,
        out_shape=(
            jax.ShapeDtypeStruct((NX, NY, NZ), f32),
            jax.ShapeDtypeStruct((NX, GR, 2 * NZ), f32),
            jax.ShapeDtypeStruct((NX, GR, 2 * NZ), i32),
        ),
        in_specs=[vmem] * 7 + [smem, vmem],
        out_specs=(vmem, vmem, vmem),
        scratch_shapes=[
            pltpu.VMEM((2, EX, EY, NZ), f32),
            pltpu.VMEM((6, EX, EY, NZ), f32),
            pltpu.VMEM((6, EX, 8, NZ), f32),
            pltpu.VMEM((EX, 8, NZ), f32),
            pltpu.VMEM((EX, 8, NZ), f32),
            pltpu.VMEM((EX, 8, NZ), f32),
            pltpu.VMEM((NX, NY, NZ), f32),
            pltpu.VMEM((NX, 8, NZ), f32),
            pltpu.VMEM((NX, 8, NZ), f32),
            pltpu.VMEM((3,) + growth, i32),
            pltpu.VMEM(growth, i32),
            pltpu.VMEM(growth, f32),
            pltpu.VMEM(growth, f32),
            pltpu.VMEM(growth, f32),
            pltpu.VMEM(growth, f32),
            pltpu.VMEM(growth, f32),
            pltpu.VMEM(growth, f32),
            dma((8,)), dma((8,)), dma, dma,
            dma((11,)), dma((3, 2)), dma((3, 2)), dma, dma((8,)), dma((8,)),
        ],
        compiler_params=pltpu.CompilerParams(
            collective_id=0, has_side_effects=True, vmem_limit_bytes=50 << 20
        ),
    )(*args)


def solution(mesh):
    thermal = P("gx", "gy", "gz")
    growth = P("gx", ("gy", "gz"), None)
    placed = (
        thermal, thermal, thermal, growth, growth, growth,
        P(None, "gx", ("gy", "gz"), None), growth, P(),
    )
    return jax.shard_map(
        body, mesh=mesh, in_specs=placed, out_specs=(thermal, growth, growth), check_vma=False
    )
```

```python
import functools

import jax
import jax.numpy as jnp
from jax import lax
from jax.experimental import pallas as pl
from jax.experimental.pallas import tpu as pltpu
from jax.sharding import PartitionSpec as P

MESH = pl.DeviceIdType.MESH
D = 6
NX, NY, NZ = 16, 32, 128
EX = NX + 2 * D
OY = 8
EY = NY + 2 * OY
PITCH = 3 * D
GR = 16
GX = NX + 4
GY = GR + 16
TINY = 1e-30


def lanes(shape):
    return lax.broadcasted_iota(jnp.int32, shape, 1)


def rows(shape):
    return lax.broadcasted_iota(jnp.int32, shape, 0)


def clip03(heat):
    return jnp.minimum(jnp.maximum(heat, 0.0), 3.0)


def state(heat, base):
    solid = clip03(heat)
    return heat - solid * (2.0 / 3.0), base * (1.0 + solid * (1.0 / 6.0))


def face(temp, cond, temp_next, cond_next):
    total = jnp.maximum(cond + cond_next, TINY)
    return (cond * cond_next) * pltpu.reciprocal(total, approx=True) * (temp_next - temp)


def roll(value, amount, axis):
    return pltpu.roll(value, amount % value.shape[axis], axis)


def shifted(value, amount, axis):
    return roll(value, amount, value.ndim - 2 + axis)


def substep(src, dst, base, step, finish=None):
    first, count = step, EX - 2 * step
    lane_end = lanes((EY, NZ)) == NZ - 1
    before_t, before_k = state(src[first - 1], base[first - 1])
    here_t, here_k = state(src[first], base[first])
    into = face(before_t, before_k, here_t, here_k)

    def slab(x, carry):
        here_t, here_k, into = carry
        next_t, next_k = state(src[x + 1], base[x + 1])
        out_of = face(here_t, here_k, next_t, next_k)
        along_y = face(here_t, here_k, roll(here_t, -1, 0), roll(here_k, -1, 0))
        along_z = face(here_t, here_k, roll(here_t, -1, 1), roll(here_k, -1, 1))
        along_z = jnp.where(lane_end, 0.0, along_z)
        total = (out_of - into) + (along_y - roll(along_y, 1, 0)) + (along_z - roll(along_z, 1, 1))
        heat = src[x] + 0.2 * total
        if finish is None:
            dst[x] = heat
        else:
            finish(x, here_t, heat)
        return next_t, next_k, out_of

    chunk = count // 2

    def several(i, carry):
        for j in range(chunk):
            carry = slab(first + chunk * i + j, carry)
        return carry

    lax.fori_loop(0, 2, several, (here_t, here_k, into))


def strip_substep(heat, base, step):
    temp, cond = state(heat, base)
    across = face(temp[:-1], cond[:-1], temp[1:], cond[1:])
    temp, cond = temp[1:-1], cond[1:-1]
    row = lax.broadcasted_iota(jnp.int32, temp.shape, 1)

    def up(v):
        turned = roll(v, -1, 1)
        return jnp.where(row == 7, roll(turned, -PITCH, 2), turned)

    def down(v):
        turned = roll(v, 1, 1)
        return jnp.where(row == 0, roll(turned, PITCH, 2), turned)

    along_y = face(temp, cond, up(temp), up(cond))
    along_z = face(temp, cond, roll(temp, -1, 2), roll(cond, -1, 2))
    total = (across[1:] - across[:-1]) + (along_y - down(along_y)) + (along_z - roll(along_z, 1, 2))
    return heat[1:-1] + 0.2 * total, temp


def outcome(earlier, temp_before, heat):
    solid = clip03(heat)
    temp = heat - solid * (2.0 / 3.0)
    liquid = solid
    for past in earlier:
        liquid = liquid + clip03(past)
    cooling = (temp_before - temp) * 10.0
    under = jnp.maximum(cooling, 0.0) * (0.5 + liquid * (0.1 / 3.0))
    return temp, under * under


def shift_z(low, high):
    lane = lanes(low.shape)
    low_down, high_down = roll(low, 1, 1), roll(high, 1, 1)
    low_up, high_up = roll(low, -1, 1), roll(high, -1, 1)
    zero = jnp.zeros_like(low)
    down = (jnp.where(lane == 0, zero, low_down), jnp.where(lane == 0, low_down, high_down))
    up = (jnp.where(lane == NZ - 1, high_up, low_up), jnp.where(lane == NZ - 1, zero, high_up))
    return down, up


def pick(ref, x, first, count, codes):
    here = (ref[0, x, pl.ds(first, count)], ref[1, x, pl.ds(first, count)])
    down, up = shift_z(*here)
    picked = []
    for half in range(2):
        code = codes[half]
        views = (
            ref[half, x - 1, pl.ds(first, count)],
            ref[half, x + 1, pl.ds(first, count)],
            ref[half, x, pl.ds(first - 1, count)],
            ref[half, x, pl.ds(first + 1, count)],
            down[half],
            up[half],
        )
        value = jnp.zeros_like(here[half])
        for number, view in enumerate(views):
            value = jnp.where(code == number + 1, view, value)
        picked.append(value)
    return picked


def loop(start, stop, unroll, step):
    assert (stop - start) % unroll == 0

    def several(i, _):
        for j in range(unroll):
            step(start + unroll * i + j)
        return 0

    lax.fori_loop(0, (stop - start) // unroll, several, 0)


def reach_rows(turns):
    cos_a, sin_a = jnp.cos(turns[0:1]), jnp.sin(turns[0:1])
    cos_b, sin_b = jnp.cos(turns[1:2]), jnp.sin(turns[1:2])
    cos_c, sin_c = jnp.cos(turns[2:3]), jnp.sin(turns[2:3])
    row_x = (
        jnp.abs(cos_a * cos_c - sin_a * sin_c * cos_b)
        + jnp.abs(-cos_a * sin_c - sin_a * cos_c * cos_b)
        + jnp.abs(sin_a * sin_b)
    )
    row_y = (
        jnp.abs(sin_a * cos_c + cos_a * sin_c * cos_b)
        + jnp.abs(-sin_a * sin_c + cos_a * cos_c * cos_b)
        + jnp.abs(-cos_a * sin_b)
    )
    row_z = jnp.abs(sin_c * sin_b) + jnp.abs(cos_c * sin_b) + jnp.abs(cos_b)
    return row_x, row_y, row_z


def lookup(tables, side, code):
    pose = side & 63
    axis = jnp.maximum(code - 1, 0) >> 1
    parts = []
    for tile in range(side.shape[0] // 8):
        cut = slice(8 * tile, 8 * tile + 8)
        index = pose[cut] + ((axis[cut] & 1) << 6)
        xy = jnp.take_along_axis(tables[0], index, axis=1, mode="promise_in_bounds")
        z = jnp.take_along_axis(tables[1], index, axis=1, mode="promise_in_bounds")
        parts.append(jnp.where(axis[cut] == 2, z, xy))
    return jnp.concatenate(parts, axis=0)


def kernel(
    kelvin_hbm, conductance_hbm, melted_hbm, germ_hbm, nucleus_hbm, pose_hbm, captured_hbm,
    roster_hbm, turns_hbm,
    temp_out, env_out, grain_out,
    kelvin, conductance, melted, germ, nucleus, pose, captured, roster, turns, load_sem,
    temp_own, env_own, grain_own, save_sem,
    bricks, history, strip_h, strip_b, strip_out, strip_in, speed,
    strip_t, strip_s, lab, lab1, reach1, reach2, gspeed, grown, grown1, env1,
    heat_send, heat_recv, strip_send, strip_recv,
    speed_send, speed_recv_a, speed_recv_b, local_sem, lab_send, lab_recv,
):
    gx, gy, gz = (lax.axis_index(a) for a in ("gx", "gy", "gz"))
    ngx, ngy = lax.axis_size("gx"), lax.axis_size("gy")

    def at(dx, dy, z):
        return (lax.rem(gx + dx + ngx, ngx), lax.rem(gy + dy + ngy, ngy), z)

    other = 1 - gz
    cross = 2 * gz - 1
    xy = [(dx, dy) for dx in (-1, 0, 1) for dy in (-1, 0, 1) if (dx, dy) != (0, 0)]
    greeted = [at(dx, dy, gz) for dx, dy in xy]
    greeted += [at(dx, 0, other) for dx in (-1, 0, 1)]
    greeted += [at(dx, cross, other) for dx in (-1, 0, 1)]
    barrier = pltpu.get_barrier_semaphore()
    for device in greeted:
        pl.semaphore_signal(barrier, inc=1, device_id=device, device_id_type=MESH)

    loads = [
        pltpu.make_async_copy(src, dst, load_sem.at[i])
        for i, (src, dst) in enumerate((
            (kelvin_hbm, kelvin), (melted_hbm, melted), (conductance_hbm, conductance),
            (germ_hbm, germ), (nucleus_hbm, nucleus), (pose_hbm, pose),
            (captured_hbm, captured), (roster_hbm, roster), (turns_hbm, turns),
        ))
    ]
    for load in loads:
        load.start()

    def send(src, dst, send_sem, recv_sem, device):
        copy = pltpu.make_async_remote_copy(
            src_ref=src, dst_ref=dst, send_sem=send_sem, recv_sem=recv_sem,
            device_id=device, device_id_type=MESH,
        )
        copy.start()
        return copy

    own_rows = pl.ds(OY, NY)

    def opening(x):
        melt = melted[x].astype(jnp.float32)
        start = kelvin[x] + 1.5 * melt
        bricks[0, D + x, own_rows] = start + 2.0 * jnp.clip(start, 0.0, 1.0)
        bricks[1, D + x, own_rows] = conductance[x] * (0.25 + 0.75 * melt)

    for load in loads[:3]:
        load.wait()
    loop(0, NX, 4, opening)

    for load in loads[3:]:
        load.wait()
    tiles = [roster[0, 0, i] for i in range(8)]

    def seeds(x):
        tile = x // 2
        active = tiles[0] == tile
        for number in tiles[1:]:
            active = jnp.logical_or(active, number == tile)
        for half in range(2):
            cut = pl.ds(half * NZ, NZ)
            label = germ[x, :, cut] * (nucleus[x, :, cut] * 64 + pose[x, :, cut])
            lab[0, half, 2 + x, pl.ds(8, GR)] = label
            for g in range(2):
                lab[1 + g, half, 2 + x, pl.ds(8, GR)] = jnp.where(
                    active, captured[g, x, :, cut], -1
                )

    loop(0, NX, 2, seeds)

    pl.semaphore_wait(barrier, len(greeted))

    copies = []
    for i, (dx, dy) in enumerate(xy):
        deep = D if dx == 0 or dy == 0 else D - 1
        src_x = {-1: (D, deep), 0: (D, NX), 1: (D + NX - deep, deep)}[dx]
        dst_x = {-1: D + NX, 0: D, 1: D - deep}[dx]
        src_y = {-1: (OY, deep), 0: (OY, NY), 1: (OY + NY - deep, deep)}[dy]
        dst_y = {-1: OY + NY, 0: OY, 1: OY - deep}[dy]
        copies.append(send(
            bricks.at[:, pl.ds(*src_x), pl.ds(*src_y)],
            bricks.at[:, pl.ds(dst_x, src_x[1]), pl.ds(dst_y, src_y[1])],
            heat_send.at[i], heat_recv.at[i], at(dx, dy, gz),
        ))

    lab_copies = []
    for i, (dx, dg) in enumerate(xy):
        deep = 2 if dx == 0 or dg == 0 else 1
        src_x = {-1: (2, deep), 0: (2, NX), 1: (2 + NX - deep, deep)}[dx]
        dst_x = {-1: 2 + NX, 0: 2, 1: 2 - deep}[dx]
        src_y = {-1: (8, deep), 0: (8, GR), 1: (8 + GR - deep, deep)}[dg]
        dst_y = {-1: 8 + GR, 0: 8, 1: 8 - deep}[dg]
        if dg == 0:
            device = at(dx, 0, gz)
        elif dg == 1:
            device = at(dx, gz, other)
        else:
            device = at(dx, gz - 1, other)
        lab_copies.append(send(
            lab.at[pl.ds(0, 2), :, pl.ds(*src_x), pl.ds(*src_y)],
            lab.at[pl.ds(0, 2), :, pl.ds(dst_x, src_x[1]), pl.ds(dst_y, src_y[1])],
            lab_send.at[i], lab_recv.at[i], device,
        ))

    row_x, row_y, row_z = reach_rows(turns[...])
    tables = [
        jnp.broadcast_to(jnp.concatenate(pair, axis=1), (8, NZ))
        for pair in ((row_x, row_y), (row_z, row_z))
    ]

    for copy in copies:
        copy.wait()

    lane8 = lanes((8, NZ))
    row_all = rows((EY, NZ))
    outside_y = ((row_all < OY) & (gy == 0)) | ((row_all >= OY + NY) & (gy == ngy - 1))
    slot = lane8
    for tile in range(1, EY // 8):
        slot = jnp.where(lane8 >= tile * PITCH, lane8 - tile * PITCH, slot)
    in_use = lane8 < PITCH * (EY // 8)
    own_slot = (slot >= D * gz) & (slot < D * gz + 2 * D)
    halo_slot = jnp.logical_not(own_slot) & in_use
    turn = D * (1 - 2 * gz)

    def pack(x):
        outside_x = ((x < D) & (gx == 0)) | ((x >= D + NX) & (gx == ngx - 1))
        base = jnp.where(outside_x | outside_y, 0.0, bricks[1, x])
        bricks[1, x] = base
        heat = bricks[0, x]
        history[0, x] = heat
        packed = []
        for value in (heat, base):
            strip = jnp.zeros((8, NZ), jnp.float32)
            for tile in range(EY // 8):
                moved = pltpu.roll(
                    value[8 * tile : 8 * tile + 8], (PITCH * tile + 2 * D - D * gz) % NZ, 1
                )
                mine = own_slot & (lane8 >= tile * PITCH) & (lane8 < (tile + 1) * PITCH)
                strip = jnp.where(mine, moved, strip)
            packed.append(strip)
        strip_h[x] = packed[0]
        strip_b[x] = packed[1]
        strip_out[x] = jnp.where(halo_slot, pltpu.roll(packed[1], (turn + NZ) % NZ, 1), packed[0])

    loop(0, EX, 4, pack)
    strip_copy = send(
        strip_out, strip_in, strip_send, strip_recv, at(0, 0, other)
    )

    for step in range(1, 6):
        substep(history.at[step - 1], history.at[step], bricks.at[1], step)

    strip_copy.wait()

    def unpack(x):
        got = strip_in[x]
        strip_h[x] = jnp.where(halo_slot, pltpu.roll(got, (turn + NZ) % NZ, 1), strip_h[x])
        strip_b[x] = jnp.where(halo_slot, pltpu.roll(got, (2 * turn + NZ) % NZ, 1), strip_b[x])

    loop(0, EX, 14, unpack)
    heat = strip_h[...]
    earlier = []
    for step in range(1, 7):
        heat, temp_before = strip_substep(heat, strip_b[pl.ds(step - 1, EX + 2 - 2 * step)], step)
        if step < 6:
            earlier.append(heat[D - step : D - step + NX])
    strip_t[...], strip_s[...] = outcome(earlier, temp_before, heat)

    near = jnp.where(gz == 0, lane8 - (NZ - D), D - 1 - lane8) >= 0

    def brick_end(x, temp_before, heat):
        temp, fast = outcome([history[s, x] for s in range(1, 6)], temp_before, heat)
        for tile in range(NY // 8):
            cut = slice(OY + 8 * tile, OY + 8 * tile + 8)
            back = (NZ - 2 * D + D * gz - PITCH * (tile + 1) + NZ) % NZ
            put = pl.ds(8 * tile, 8)
            temp_own[x - D, put] = jnp.where(
                near, pltpu.roll(strip_t[x - D], back, 1), temp[cut]
            )
            speed[x - D, put] = jnp.where(
                near, pltpu.roll(strip_s[x - D], back, 1), fast[cut]
            )

    substep(history.at[5], None, bricks.at[1], 6, brick_end)
    temp_save = pltpu.make_async_copy(temp_own, temp_out, save_sem.at[0])
    temp_save.start()

    speed_copies = []

    def tell(dx, dy, z, number, recv_sem):
        if dy == 0:
            deep_x = 2
            src_y, dst_y, count_y = 14 * z, 8 - 2 * z, 18
        else:
            deep_x = 1
            count_y = 2 if dx == 0 else 1
            src_y = NY - count_y if dy == 1 else 0
            dst_y = 8 - count_y if dy == 1 else 8 + GR
        src_x = {-1: (0, deep_x), 0: (0, NX), 1: (NX - deep_x, deep_x)}[dx]
        dst_x = {-1: 2 + NX, 0: 2, 1: 2 - deep_x}[dx]
        speed_copies.append(send(
            speed.at[pl.ds(*src_x), pl.ds(src_y, count_y)],
            gspeed.at[gz, pl.ds(dst_x, src_x[1]), pl.ds(dst_y, count_y)],
            speed_send.at[number], recv_sem, at(dx, dy, z),
        ))

    for dx in (-1, 1):
        for z in range(2):
            tell(dx, 0, z, len(speed_copies), speed_recv_a.at[dx + 1, gz])
    for dy, z in ((1, 0), (-1, 1)):
        for dx in (-1, 0, 1):
            tell(dx, dy, z, len(speed_copies), speed_recv_b.at[dx + 1, gz])
    tell(0, 0, other, len(speed_copies), speed_recv_a.at[1, gz])
    keep = pltpu.make_async_copy(
        speed.at[:, pl.ds(14 * gz, 18)],
        gspeed.at[gz, pl.ds(2, NX), pl.ds(8 - 2 * gz, 18)],
        local_sem,
    )
    keep.start()

    for copy in lab_copies:
        copy.wait()
    row_g = rows((GY, NZ))
    outside_g = ((row_g < 8) & (gy + gz == 0)) | (
        (row_g >= 8 + GR) & (gy + gz == ngy)
    )

    def border(x):
        outside = outside_g | ((x < 2) & (gx == 0)) | ((x >= 2 + NX) & (gx == ngx - 1))
        for half in range(2):
            lab[0, half, x] = jnp.where(outside, 0, lab[0, half, x])
            lab[1, half, x] = jnp.where(outside, -1, lab[1, half, x])

    loop(0, GX, 2, border)
    wide = pl.ds(7, 24)
    own = pl.ds(8, GR)

    def first_labels(x):
        codes = [lab[1, half, x, wide] for half in range(2)]
        sides = pick(lab.at[0], x, 7, 24, codes)
        for half in range(2):
            lab1[half, x, wide] = jnp.where(codes[half] > 0, sides[half], lab[0, half, x, wide])
            reach1[half, x, wide] = lookup(tables, sides[half], codes[half])

    loop(1, GX - 1, 3, first_labels)

    def second_labels(x):
        codes = [lab[2, half, x, own] for half in range(2)]
        sides = pick(lab1, x, 8, GR, codes)
        for half in range(2):
            label = jnp.where(codes[half] > 0, sides[half], lab1[half, x, own])
            grain_own[x - 2, :, pl.ds(half * NZ, NZ)] = label >> 6
            reach2[half, x, own] = lookup(tables, sides[half], codes[half])

    loop(2, GX - 2, 4, second_labels)
    grain_save = pltpu.make_async_copy(grain_own, grain_out, save_sem.at[1])
    grain_save.start()

    for copy in speed_copies:
        copy.wait_send()
    keep.wait()

    def heard(count_x, count_y, recv_sem):
        pltpu.make_async_remote_copy(
            src_ref=speed.at[pl.ds(0, count_x), pl.ds(0, count_y)],
            dst_ref=gspeed.at[0, pl.ds(0, count_x), pl.ds(0, count_y)],
            send_sem=speed_send.at[0], recv_sem=recv_sem,
            device_id=at(0, 0, other), device_id_type=MESH,
        ).wait_recv()

    for z in range(2):
        for dx in (-1, 1):
            heard(2, 18, speed_recv_a.at[dx + 1, z])
            heard(1, 1, speed_recv_b.at[dx + 1, z])
        heard(NX, 2, speed_recv_b.at[1, z])
    heard(NX, 18, speed_recv_a.at[1, other])

    def seeded(x):
        for half in range(2):
            grown[half, x] = jnp.where(lab[0, half, x] > 0, gspeed[half, x], 0.0)

    loop(0, GX, 4, seeded)

    def first_growth(x):
        codes = [lab[1, half, x, wide] for half in range(2)]
        sides = pick(grown, x, 7, 24, codes)
        for half in range(2):
            code = codes[half]
            caught = jnp.maximum(sides[half] - reach1[half, x, wide], 0.0)
            envelope = jnp.where(
                code > 0, caught, jnp.where(code == 0, grown[half, x, wide], 0.0)
            )
            env1[half, x, wide] = envelope
            grown1[half, x, wide] = envelope + jnp.where(
                lab1[half, x, wide] > 0, gspeed[half, x, wide], 0.0
            )

    loop(1, GX - 1, 3, first_growth)

    def second_growth(x):
        codes = [lab[2, half, x, own] for half in range(2)]
        sides = pick(grown1, x, 8, GR, codes)
        for half in range(2):
            code = codes[half]
            caught = jnp.maximum(sides[half] - reach2[half, x, own], 0.0)
            kept = jnp.where(code == 0, grown1[half, x, own], env1[half, x, own])
            env_own[x - 2, :, pl.ds(half * NZ, NZ)] = jnp.where(code > 0, caught, kept)

    loop(2, GX - 2, 4, second_growth)
    env_save = pltpu.make_async_copy(env_own, env_out, save_sem.at[2])
    env_save.start()
    for save in (temp_save, grain_save, env_save):
        save.wait()


def handing_on(*refs):
    sources, targets, held, sems = refs[:3], refs[3:6], refs[6:9], refs[9]
    fetches = [pltpu.make_async_copy(sources[i], held[i], sems.at[0, i]) for i in range(3)]
    stores = [pltpu.make_async_copy(held[i], targets[i], sems.at[1, i]) for i in range(3)]
    for fetch in fetches:
        fetch.start()
    for fetch, store in zip(fetches, stores):
        fetch.wait()
        store.start()
    for store in stores:
        store.wait()


def body(*args):
    hbm = pl.BlockSpec(memory_space=pltpu.HBM)
    f32, i32 = jnp.float32, jnp.int32
    dma = pltpu.SemaphoreType.DMA
    growth = (2, GX, GY, NZ)
    results = (
        jax.ShapeDtypeStruct((NX, NY, NZ), f32),
        jax.ShapeDtypeStruct((NX, GR, 2 * NZ), f32),
        jax.ShapeDtypeStruct((NX, GR, 2 * NZ), i32),
    )
    made = pl.pallas_call(
        kernel,
        out_shape=results,
        in_specs=[hbm] * 9,
        out_specs=(hbm, hbm, hbm),
        scratch_shapes=[
            pltpu.VMEM((NX, NY, NZ), f32),
            pltpu.VMEM((NX, NY, NZ), f32),
            pltpu.VMEM((NX, NY, NZ), i32),
            pltpu.VMEM((NX, GR, 2 * NZ), i32),
            pltpu.VMEM((NX, GR, 2 * NZ), i32),
            pltpu.VMEM((NX, GR, 2 * NZ), i32),
            pltpu.VMEM((2, NX, GR, 2 * NZ), i32),
            pltpu.SMEM((1, 1, 8), i32),
            pltpu.VMEM((3, 64), f32),
            dma((9,)),
            pltpu.VMEM((NX, NY, NZ), f32),
            pltpu.VMEM((NX, GR, 2 * NZ), f32),
            pltpu.VMEM((NX, GR, 2 * NZ), i32),
            dma((3,)),
            pltpu.VMEM((2, EX, EY, NZ), f32),
            pltpu.VMEM((6, EX, EY, NZ), f32),
            pltpu.VMEM((EX, 8, NZ), f32),
            pltpu.VMEM((EX, 8, NZ), f32),
            pltpu.VMEM((EX, 8, NZ), f32),
            pltpu.VMEM((EX, 8, NZ), f32),
            pltpu.VMEM((NX, NY, NZ), f32),
            pltpu.VMEM((NX, 8, NZ), f32),
            pltpu.VMEM((NX, 8, NZ), f32),
            pltpu.VMEM((3,) + growth, i32),
            pltpu.VMEM(growth, i32),
            pltpu.VMEM(growth, f32),
            pltpu.VMEM(growth, f32),
            pltpu.VMEM(growth, f32),
            pltpu.VMEM(growth, f32),
            pltpu.VMEM(growth, f32),
            pltpu.VMEM(growth, f32),
            dma((8,)), dma((8,)), dma, dma,
            dma((11,)), dma((3, 2)), dma((3, 2)), dma, dma((8,)), dma((8,)),
        ],
        compiler_params=pltpu.CompilerParams(
            collective_id=0, has_side_effects=True, vmem_limit_bytes=62 << 20
        ),
    )(*args)
    return pl.pallas_call(
        handing_on,
        out_shape=results,
        in_specs=[hbm] * 3,
        out_specs=(hbm, hbm, hbm),
        scratch_shapes=[pltpu.VMEM(r.shape, r.dtype) for r in results] + [dma((2, 3))],
        compiler_params=pltpu.CompilerParams(vmem_limit_bytes=62 << 20),
    )(*made)


def solution(mesh):
    thermal = P("gx", "gy", "gz")
    growth = P("gx", ("gy", "gz"), None)
    placed = (
        thermal, thermal, thermal, growth, growth, growth,
        P(None, "gx", ("gy", "gz"), None), growth, P(),
    )
    return jax.shard_map(
        body, mesh=mesh, in_specs=placed, out_specs=(thermal, growth, growth), check_vma=False
    )
```

```python
import functools

import jax
import jax.numpy as jnp
from jax import lax
from jax.experimental import pallas as pl
from jax.experimental.pallas import tpu as pltpu
from jax.sharding import PartitionSpec as P

MESH = pl.DeviceIdType.MESH
D = 6
NX, NY, NZ = 16, 32, 128
EX = NX + 2 * D
OY = 8
EY = NY + 2 * OY
PITCH = 3 * D
GR = 16
GX = NX + 4
GY = GR + 16
TINY = 1e-30


def lanes(shape):
    return lax.broadcasted_iota(jnp.int32, shape, 1)


def rows(shape):
    return lax.broadcasted_iota(jnp.int32, shape, 0)


def clip03(heat):
    return jnp.minimum(jnp.maximum(heat, 0.0), 3.0)


def state(heat, base):
    solid = clip03(heat)
    return heat - solid * (2.0 / 3.0), base * (1.0 + solid * (1.0 / 6.0))


def face(temp, cond, temp_next, cond_next):
    total = jnp.maximum(cond + cond_next, TINY)
    return (cond * cond_next) * pltpu.reciprocal(total, approx=True) * (temp_next - temp)


def roll(value, amount, axis):
    return pltpu.roll(value, amount % value.shape[axis], axis)


def shifted(value, amount, axis):
    return roll(value, amount, value.ndim - 2 + axis)


def substep(src, dst, base, step, finish=None):
    first, count = step, EX - 2 * step
    lane_end = lanes((EY, NZ)) == NZ - 1
    before_t, before_k = state(src[first - 1], base[first - 1])
    here_t, here_k = state(src[first], base[first])
    into = face(before_t, before_k, here_t, here_k)

    def slab(x, carry):
        here_t, here_k, into = carry
        next_t, next_k = state(src[x + 1], base[x + 1])
        out_of = face(here_t, here_k, next_t, next_k)
        along_y = face(here_t, here_k, roll(here_t, -1, 0), roll(here_k, -1, 0))
        along_z = face(here_t, here_k, roll(here_t, -1, 1), roll(here_k, -1, 1))
        along_z = jnp.where(lane_end, 0.0, along_z)
        total = (out_of - into) + (along_y - roll(along_y, 1, 0)) + (along_z - roll(along_z, 1, 1))
        heat = src[x] + 0.2 * total
        if finish is None:
            dst[x] = heat
        else:
            finish(x, here_t, heat)
        return next_t, next_k, out_of

    chunk = count // 2

    def several(i, carry):
        for j in range(chunk):
            carry = slab(first + chunk * i + j, carry)
        return carry

    lax.fori_loop(0, 2, several, (here_t, here_k, into))


def last_rows(before, history, base, first):
    near, own = pl.ds(first, 8), pl.ds(D, NX)
    heat = before[pl.ds(D - 1, NX + 2), near]
    temp, cond = state(heat, base[pl.ds(D - 1, NX + 2), near])
    across = face(temp[:-1], cond[:-1], temp[1:], cond[1:])
    temp, cond = temp[1:-1], cond[1:-1]
    lane_end = lax.broadcasted_iota(jnp.int32, temp.shape, 2) == NZ - 1
    along_y = face(temp, cond, roll(temp, -1, 1), roll(cond, -1, 1))
    along_z = face(temp, cond, roll(temp, -1, 2), roll(cond, -1, 2))
    along_z = jnp.where(lane_end, 0.0, along_z)
    total = (
        (across[1:] - across[:-1])
        + (along_y - roll(along_y, 1, 1))
        + (along_z - roll(along_z, 1, 2))
    )
    earlier = [history[s, own, near] for s in range(1, 6)]
    return outcome(earlier, temp, heat[1:-1] + 0.2 * total)[1]


def strip_substep(heat, base, step):
    temp, cond = state(heat, base)
    across = face(temp[:-1], cond[:-1], temp[1:], cond[1:])
    temp, cond = temp[1:-1], cond[1:-1]
    row = lax.broadcasted_iota(jnp.int32, temp.shape, 1)

    def up(v):
        turned = roll(v, -1, 1)
        return jnp.where(row == 7, roll(turned, -PITCH, 2), turned)

    def down(v):
        turned = roll(v, 1, 1)
        return jnp.where(row == 0, roll(turned, PITCH, 2), turned)

    along_y = face(temp, cond, up(temp), up(cond))
    along_z = face(temp, cond, roll(temp, -1, 2), roll(cond, -1, 2))
    total = (across[1:] - across[:-1]) + (along_y - down(along_y)) + (along_z - roll(along_z, 1, 2))
    return heat[1:-1] + 0.2 * total, temp


def outcome(earlier, temp_before, heat):
    solid = clip03(heat)
    temp = heat - solid * (2.0 / 3.0)
    liquid = solid
    for past in earlier:
        liquid = liquid + clip03(past)
    cooling = (temp_before - temp) * 10.0
    under = jnp.maximum(cooling, 0.0) * (0.5 + liquid * (0.1 / 3.0))
    return temp, under * under


def shift_z(low, high):
    lane = lanes(low.shape)
    low_down, high_down = roll(low, 1, 1), roll(high, 1, 1)
    low_up, high_up = roll(low, -1, 1), roll(high, -1, 1)
    zero = jnp.zeros_like(low)
    down = (jnp.where(lane == 0, zero, low_down), jnp.where(lane == 0, low_down, high_down))
    up = (jnp.where(lane == NZ - 1, high_up, low_up), jnp.where(lane == NZ - 1, zero, high_up))
    return down, up


def pick(ref, x, first, count, codes):
    here = (ref[0, x, pl.ds(first, count)], ref[1, x, pl.ds(first, count)])
    down, up = shift_z(*here)
    picked = []
    for half in range(2):
        code = codes[half]
        views = (
            ref[half, x - 1, pl.ds(first, count)],
            ref[half, x + 1, pl.ds(first, count)],
            ref[half, x, pl.ds(first - 1, count)],
            ref[half, x, pl.ds(first + 1, count)],
            down[half],
            up[half],
        )
        value = jnp.zeros_like(here[half])
        for number, view in enumerate(views):
            value = jnp.where(code == number + 1, view, value)
        picked.append(value)
    return picked


def loop(start, stop, unroll, step):
    assert (stop - start) % unroll == 0

    def several(i, _):
        for j in range(unroll):
            step(start + unroll * i + j)
        return 0

    lax.fori_loop(0, (stop - start) // unroll, several, 0)


def reach_rows(turns):
    cos_a, sin_a = jnp.cos(turns[0:1]), jnp.sin(turns[0:1])
    cos_b, sin_b = jnp.cos(turns[1:2]), jnp.sin(turns[1:2])
    cos_c, sin_c = jnp.cos(turns[2:3]), jnp.sin(turns[2:3])
    row_x = (
        jnp.abs(cos_a * cos_c - sin_a * sin_c * cos_b)
        + jnp.abs(-cos_a * sin_c - sin_a * cos_c * cos_b)
        + jnp.abs(sin_a * sin_b)
    )
    row_y = (
        jnp.abs(sin_a * cos_c + cos_a * sin_c * cos_b)
        + jnp.abs(-sin_a * sin_c + cos_a * cos_c * cos_b)
        + jnp.abs(-cos_a * sin_b)
    )
    row_z = jnp.abs(sin_c * sin_b) + jnp.abs(cos_c * sin_b) + jnp.abs(cos_b)
    return row_x, row_y, row_z


def lookup(tables, side, code):
    pose = side & 63
    axis = jnp.maximum(code - 1, 0) >> 1
    parts = []
    for tile in range(side.shape[0] // 8):
        cut = slice(8 * tile, 8 * tile + 8)
        index = pose[cut] + ((axis[cut] & 1) << 6)
        xy = jnp.take_along_axis(tables[0], index, axis=1, mode="promise_in_bounds")
        z = jnp.take_along_axis(tables[1], index, axis=1, mode="promise_in_bounds")
        parts.append(jnp.where(axis[cut] == 2, z, xy))
    return jnp.concatenate(parts, axis=0)


def kernel(
    kelvin_hbm, conductance_hbm, melted_hbm, germ_hbm, nucleus_hbm, pose_hbm, captured_hbm,
    roster_hbm, turns_hbm,
    temp_out, env_out, grain_out,
    kelvin, conductance, melted, germ, nucleus, pose, captured, roster, turns, load_sem,
    temp_own, env_own, grain_own, save_sem,
    bricks, history, strip_h, strip_b, strip_out, strip_in, speed,
    far, strip_t, strip_s, lab, lab1, reach1, reach2, gspeed, grown, grown1, env1,
    heat_send, heat_recv, strip_send, strip_recv,
    speed_send, speed_recv_a, speed_recv_b, local_sem, lab_send, lab_recv,
):
    gx, gy, gz = (lax.axis_index(a) for a in ("gx", "gy", "gz"))
    ngx, ngy = lax.axis_size("gx"), lax.axis_size("gy")

    def at(dx, dy, z):
        return (lax.rem(gx + dx + ngx, ngx), lax.rem(gy + dy + ngy, ngy), z)

    other = 1 - gz
    cross = 2 * gz - 1
    xy = [(0, -1), (0, 1), (-1, -1), (1, 1), (-1, 1), (1, -1), (-1, 0), (1, 0)]
    greeted = [at(dx, dy, gz) for dx, dy in xy]
    greeted += [at(dx, 0, other) for dx in (-1, 0, 1)]
    greeted += [at(dx, cross, other) for dx in (-1, 0, 1)]
    barrier = pltpu.get_barrier_semaphore()
    for device in greeted:
        pl.semaphore_signal(barrier, inc=1, device_id=device, device_id_type=MESH)

    loads = [
        pltpu.make_async_copy(src, dst, load_sem.at[i])
        for i, (src, dst) in enumerate((
            (kelvin_hbm, kelvin), (melted_hbm, melted), (conductance_hbm, conductance),
            (germ_hbm, germ), (nucleus_hbm, nucleus), (pose_hbm, pose),
            (captured_hbm, captured), (roster_hbm, roster), (turns_hbm, turns),
        ))
    ]
    for load in loads:
        load.start()

    def send(src, dst, send_sem, recv_sem, device):
        copy = pltpu.make_async_remote_copy(
            src_ref=src, dst_ref=dst, send_sem=send_sem, recv_sem=recv_sem,
            device_id=device, device_id_type=MESH,
        )
        copy.start()
        return copy

    own_rows = pl.ds(OY, NY)

    def opening(x):
        melt = melted[x].astype(jnp.float32)
        start = kelvin[x] + 1.5 * melt
        bricks[0, D + x, own_rows] = start + 2.0 * jnp.clip(start, 0.0, 1.0)
        bricks[1, D + x, own_rows] = conductance[x] * (0.25 + 0.75 * melt)

    for load in loads[:3]:
        load.wait()
    loop(0, NX, 4, opening)

    for load in loads[3:]:
        load.wait()
    tiles = [roster[0, 0, i] for i in range(8)]

    def seeds(x):
        tile = x // 2
        active = tiles[0] == tile
        for number in tiles[1:]:
            active = jnp.logical_or(active, number == tile)
        for half in range(2):
            cut = pl.ds(half * NZ, NZ)
            label = germ[x, :, cut] * (nucleus[x, :, cut] * 64 + pose[x, :, cut])
            lab[0, half, 2 + x, pl.ds(8, GR)] = label
            for g in range(2):
                lab[1 + g, half, 2 + x, pl.ds(8, GR)] = jnp.where(
                    active, captured[g, x, :, cut], -1
                )

    loop(0, NX, 2, seeds)

    pl.semaphore_wait(barrier, len(greeted))

    copies = []
    for i, (dx, dy) in enumerate(xy):
        deep = D if dx == 0 or dy == 0 else D - 1
        src_x = {-1: (D, deep), 0: (D, NX), 1: (D + NX - deep, deep)}[dx]
        dst_x = {-1: D + NX, 0: D, 1: D - deep}[dx]
        src_y = {-1: (OY, deep), 0: (OY, NY), 1: (OY + NY - deep, deep)}[dy]
        dst_y = {-1: OY + NY, 0: OY, 1: OY - deep}[dy]
        copies.append(send(
            bricks.at[:, pl.ds(*src_x), pl.ds(*src_y)],
            bricks.at[:, pl.ds(dst_x, src_x[1]), pl.ds(dst_y, src_y[1])],
            heat_send.at[i], heat_recv.at[i], at(dx, dy, gz),
        ))

    row_x, row_y, row_z = reach_rows(turns[...])
    tables = [
        jnp.broadcast_to(jnp.concatenate(pair, axis=1), (8, NZ))
        for pair in ((row_x, row_y), (row_z, row_z))
    ]

    for copy in copies:
        copy.wait()

    lane8 = lanes((8, NZ))
    row_all = rows((EY, NZ))
    outside_y = ((row_all < OY) & (gy == 0)) | ((row_all >= OY + NY) & (gy == ngy - 1))
    slot = lane8
    for tile in range(1, EY // 8):
        slot = jnp.where(lane8 >= tile * PITCH, lane8 - tile * PITCH, slot)
    in_use = lane8 < PITCH * (EY // 8)
    own_slot = (slot >= D * gz) & (slot < D * gz + 2 * D)
    halo_slot = jnp.logical_not(own_slot) & in_use
    turn = D * (1 - 2 * gz)

    def pack(x):
        outside_x = ((x < D) & (gx == 0)) | ((x >= D + NX) & (gx == ngx - 1))
        base = jnp.where(outside_x | outside_y, 0.0, bricks[1, x])
        bricks[1, x] = base
        heat = bricks[0, x]
        packed = []
        for value in (heat, base):
            strip = jnp.zeros((8, NZ), jnp.float32)
            for tile in range(EY // 8):
                moved = pltpu.roll(
                    value[8 * tile : 8 * tile + 8], (PITCH * tile + 2 * D - D * gz) % NZ, 1
                )
                mine = own_slot & (lane8 >= tile * PITCH) & (lane8 < (tile + 1) * PITCH)
                strip = jnp.where(mine, moved, strip)
            packed.append(strip)
        strip_h[x] = packed[0]
        strip_b[x] = packed[1]
        strip_out[x] = jnp.where(halo_slot, pltpu.roll(packed[1], (turn + NZ) % NZ, 1), packed[0])

    loop(0, EX, 4, pack)
    strip_copy = send(
        strip_out, strip_in, strip_send, strip_recv, at(0, 0, other)
    )

    lab_copies = []
    for i, (dx, dg) in enumerate(xy):
        deep = 2 if dx == 0 or dg == 0 else 1
        src_x = {-1: (2, deep), 0: (2, NX), 1: (2 + NX - deep, deep)}[dx]
        dst_x = {-1: 2 + NX, 0: 2, 1: 2 - deep}[dx]
        src_y = {-1: (8, deep), 0: (8, GR), 1: (8 + GR - deep, deep)}[dg]
        dst_y = {-1: 8 + GR, 0: 8, 1: 8 - deep}[dg]
        if dg == 0:
            device = at(dx, 0, gz)
        elif dg == 1:
            device = at(dx, gz, other)
        else:
            device = at(dx, gz - 1, other)
        lab_copies.append(send(
            lab.at[pl.ds(0, 2), :, pl.ds(*src_x), pl.ds(*src_y)],
            lab.at[pl.ds(0, 2), :, pl.ds(dst_x, src_x[1]), pl.ds(dst_y, src_y[1])],
            lab_send.at[i], lab_recv.at[i], device,
        ))

    for step in range(1, 6):
        before = bricks.at[0] if step == 1 else history.at[step - 1]
        substep(before, history.at[step], bricks.at[1], step)

    strip_copy.wait()

    def unpack(x):
        got = strip_in[x]
        strip_h[x] = jnp.where(halo_slot, pltpu.roll(got, (turn + NZ) % NZ, 1), strip_h[x])
        strip_b[x] = jnp.where(halo_slot, pltpu.roll(got, (2 * turn + NZ) % NZ, 1), strip_b[x])

    loop(0, EX, 14, unpack)
    heat = strip_h[...]
    earlier = []
    for step in range(1, 7):
        heat, temp_before = strip_substep(heat, strip_b[pl.ds(step - 1, EX + 2 - 2 * step)], step)
        if step < 6:
            earlier.append(heat[D - step : D - step + NX])
    strip_t[...], strip_s[...] = outcome(earlier, temp_before, heat)

    near = jnp.where(gz == 0, lane8 - (NZ - D), D - 1 - lane8) >= 0

    speed_copies = []

    def tell(dx, dy, z, number, recv_sem):
        if dy == 0:
            deep_x = 2
            src_y, dst_y, count_y = 14 * z, 8 - 2 * z, 18
        else:
            deep_x = 1
            count_y = 2 if dx == 0 else 1
            src_y = 2 - count_y if dy == 1 else 0
            dst_y = 8 - count_y if dy == 1 else 8 + GR
        src_x = {-1: (0, deep_x), 0: (0, NX), 1: (NX - deep_x, deep_x)}[dx]
        dst_x = {-1: 2 + NX, 0: 2, 1: 2 - deep_x}[dx]
        source = speed if dy == 0 else far.at[(1 - dy) // 2]
        speed_copies.append(send(
            source.at[pl.ds(*src_x), pl.ds(src_y, count_y)],
            gspeed.at[gz, pl.ds(dst_x, src_x[1]), pl.ds(dst_y, count_y)],
            speed_send.at[number], recv_sem, at(dx, dy, z),
        ))

    turned = [
        pltpu.roll(strip_s[...], (NZ - 2 * D + D * gz - PITCH * (tile + 1) + NZ) % NZ, 2)
        for tile in (NY // 8 - 1, 0)
    ]
    near_all = jnp.broadcast_to(near[None], (NX, 8, NZ))
    upper = last_rows(history.at[5], history, bricks.at[1], OY + NY - 7)
    upper = jnp.where(near_all, turned[0], roll(upper, 1, 1))
    lower = last_rows(history.at[5], history, bricks.at[1], OY - 1)
    lower = jnp.where(near_all, turned[1], roll(lower, -1, 1))
    far[0, :, pl.ds(0, 2)] = upper[:, 6:8]
    far[1, :, pl.ds(0, 2)] = lower[:, 0:2]
    for dx in (0, -1, 1):
        for dy, z in ((1, 0), (-1, 1)):
            tell(dx, dy, z, len(speed_copies), speed_recv_b.at[dx + 1, gz])

    def brick_end(x, temp_before, heat):
        temp, fast = outcome([history[s, x] for s in range(1, 6)], temp_before, heat)
        for tile in range(NY // 8):
            cut = slice(OY + 8 * tile, OY + 8 * tile + 8)
            back = (NZ - 2 * D + D * gz - PITCH * (tile + 1) + NZ) % NZ
            put = pl.ds(8 * tile, 8)
            temp_own[x - D, put] = jnp.where(
                near, pltpu.roll(strip_t[x - D], back, 1), temp[cut]
            )
            speed[x - D, put] = jnp.where(
                near, pltpu.roll(strip_s[x - D], back, 1), fast[cut]
            )

    substep(history.at[5], None, bricks.at[1], 6, brick_end)
    temp_save = pltpu.make_async_copy(temp_own, temp_out, save_sem.at[0])
    temp_save.start()

    for dx in (-1, 1):
        for z in range(2):
            tell(dx, 0, z, len(speed_copies), speed_recv_a.at[dx + 1, gz])
    tell(0, 0, other, len(speed_copies), speed_recv_a.at[1, gz])
    keep = pltpu.make_async_copy(
        speed.at[:, pl.ds(14 * gz, 18)],
        gspeed.at[gz, pl.ds(2, NX), pl.ds(8 - 2 * gz, 18)],
        local_sem,
    )
    keep.start()

    for copy in lab_copies:
        copy.wait()
    row_g = rows((GY, NZ))
    outside_g = ((row_g < 8) & (gy + gz == 0)) | (
        (row_g >= 8 + GR) & (gy + gz == ngy)
    )

    def border(x):
        outside = outside_g | ((x < 2) & (gx == 0)) | ((x >= 2 + NX) & (gx == ngx - 1))
        for half in range(2):
            lab[0, half, x] = jnp.where(outside, 0, lab[0, half, x])
            lab[1, half, x] = jnp.where(outside, -1, lab[1, half, x])

    loop(0, GX, 2, border)
    wide = pl.ds(7, 24)
    own = pl.ds(8, GR)

    def first_labels(x):
        codes = [lab[1, half, x, wide] for half in range(2)]
        sides = pick(lab.at[0], x, 7, 24, codes)
        for half in range(2):
            lab1[half, x, wide] = jnp.where(codes[half] > 0, sides[half], lab[0, half, x, wide])
            reach1[half, x, wide] = lookup(tables, sides[half], codes[half])

    loop(1, GX - 1, 3, first_labels)

    def second_labels(x):
        codes = [lab[2, half, x, own] for half in range(2)]
        sides = pick(lab1, x, 8, GR, codes)
        for half in range(2):
            label = jnp.where(codes[half] > 0, sides[half], lab1[half, x, own])
            grain_own[x - 2, :, pl.ds(half * NZ, NZ)] = label >> 6
            reach2[half, x, own] = lookup(tables, sides[half], codes[half])

    loop(2, GX - 2, 4, second_labels)
    grain_save = pltpu.make_async_copy(grain_own, grain_out, save_sem.at[1])
    grain_save.start()

    for copy in speed_copies:
        copy.wait_send()
    keep.wait()

    def heard(count_x, count_y, recv_sem):
        pltpu.make_async_remote_copy(
            src_ref=speed.at[pl.ds(0, count_x), pl.ds(0, count_y)],
            dst_ref=gspeed.at[0, pl.ds(0, count_x), pl.ds(0, count_y)],
            send_sem=speed_send.at[0], recv_sem=recv_sem,
            device_id=at(0, 0, other), device_id_type=MESH,
        ).wait_recv()

    for z in range(2):
        for dx in (-1, 1):
            heard(2, 18, speed_recv_a.at[dx + 1, z])
            heard(1, 1, speed_recv_b.at[dx + 1, z])
        heard(NX, 2, speed_recv_b.at[1, z])
    heard(NX, 18, speed_recv_a.at[1, other])

    def seeded(x):
        for half in range(2):
            grown[half, x] = jnp.where(lab[0, half, x] > 0, gspeed[half, x], 0.0)

    loop(0, GX, 4, seeded)

    def first_growth(x):
        codes = [lab[1, half, x, wide] for half in range(2)]
        sides = pick(grown, x, 7, 24, codes)
        for half in range(2):
            code = codes[half]
            caught = jnp.maximum(sides[half] - reach1[half, x, wide], 0.0)
            envelope = jnp.where(
                code > 0, caught, jnp.where(code == 0, grown[half, x, wide], 0.0)
            )
            env1[half, x, wide] = envelope
            grown1[half, x, wide] = envelope + jnp.where(
                lab1[half, x, wide] > 0, gspeed[half, x, wide], 0.0
            )

    loop(1, GX - 1, 3, first_growth)

    def second_growth(x):
        codes = [lab[2, half, x, own] for half in range(2)]
        sides = pick(grown1, x, 8, GR, codes)
        for half in range(2):
            code = codes[half]
            caught = jnp.maximum(sides[half] - reach2[half, x, own], 0.0)
            kept = jnp.where(code == 0, grown1[half, x, own], env1[half, x, own])
            env_own[x - 2, :, pl.ds(half * NZ, NZ)] = jnp.where(code > 0, caught, kept)

    loop(2, GX - 2, 4, second_growth)
    env_save = pltpu.make_async_copy(env_own, env_out, save_sem.at[2])
    env_save.start()
    for save in (temp_save, grain_save, env_save):
        save.wait()


def handing_on(*refs):
    sources, targets, held, sems = refs[:3], refs[3:6], refs[6:9], refs[9]
    fetches = [pltpu.make_async_copy(sources[i], held[i], sems.at[0, i]) for i in range(3)]
    stores = [pltpu.make_async_copy(held[i], targets[i], sems.at[1, i]) for i in range(3)]
    for fetch in fetches:
        fetch.start()
    for fetch, store in zip(fetches, stores):
        fetch.wait()
        store.start()
    for store in stores:
        store.wait()


def body(*args):
    hbm = pl.BlockSpec(memory_space=pltpu.HBM)
    f32, i32 = jnp.float32, jnp.int32
    dma = pltpu.SemaphoreType.DMA
    growth = (2, GX, GY, NZ)
    results = (
        jax.ShapeDtypeStruct((NX, NY, NZ), f32),
        jax.ShapeDtypeStruct((NX, GR, 2 * NZ), f32),
        jax.ShapeDtypeStruct((NX, GR, 2 * NZ), i32),
    )
    made = pl.pallas_call(
        kernel,
        out_shape=results,
        in_specs=[hbm] * 9,
        out_specs=(hbm, hbm, hbm),
        scratch_shapes=[
            pltpu.VMEM((NX, NY, NZ), f32),
            pltpu.VMEM((NX, NY, NZ), f32),
            pltpu.VMEM((NX, NY, NZ), i32),
            pltpu.VMEM((NX, GR, 2 * NZ), i32),
            pltpu.VMEM((NX, GR, 2 * NZ), i32),
            pltpu.VMEM((NX, GR, 2 * NZ), i32),
            pltpu.VMEM((2, NX, GR, 2 * NZ), i32),
            pltpu.SMEM((1, 1, 8), i32),
            pltpu.VMEM((3, 64), f32),
            dma((9,)),
            pltpu.VMEM((NX, NY, NZ), f32),
            pltpu.VMEM((NX, GR, 2 * NZ), f32),
            pltpu.VMEM((NX, GR, 2 * NZ), i32),
            dma((3,)),
            pltpu.VMEM((2, EX, EY, NZ), f32),
            pltpu.VMEM((6, EX, EY, NZ), f32),
            pltpu.VMEM((EX, 8, NZ), f32),
            pltpu.VMEM((EX, 8, NZ), f32),
            pltpu.VMEM((EX, 8, NZ), f32),
            pltpu.VMEM((EX, 8, NZ), f32),
            pltpu.VMEM((NX, NY, NZ), f32),
            pltpu.VMEM((2, NX, 8, NZ), f32),
            pltpu.VMEM((NX, 8, NZ), f32),
            pltpu.VMEM((NX, 8, NZ), f32),
            pltpu.VMEM((3,) + growth, i32),
            pltpu.VMEM(growth, i32),
            pltpu.VMEM(growth, f32),
            pltpu.VMEM(growth, f32),
            pltpu.VMEM(growth, f32),
            pltpu.VMEM(growth, f32),
            pltpu.VMEM(growth, f32),
            pltpu.VMEM(growth, f32),
            dma((8,)), dma((8,)), dma, dma,
            dma((14,)), dma((3, 2)), dma((3, 2)), dma, dma((8,)), dma((8,)),
        ],
        compiler_params=pltpu.CompilerParams(
            collective_id=0, has_side_effects=True, vmem_limit_bytes=62 << 20
        ),
    )(*args)
    return pl.pallas_call(
        handing_on,
        out_shape=results,
        in_specs=[hbm] * 3,
        out_specs=(hbm, hbm, hbm),
        scratch_shapes=[pltpu.VMEM(r.shape, r.dtype) for r in results] + [dma((2, 3))],
        compiler_params=pltpu.CompilerParams(vmem_limit_bytes=62 << 20),
    )(*made)


def solution(mesh):
    thermal = P("gx", "gy", "gz")
    growth = P("gx", ("gy", "gz"), None)
    placed = (
        thermal, thermal, thermal, growth, growth, growth,
        P(None, "gx", ("gy", "gz"), None), growth, P(),
    )
    return jax.shard_map(
        body, mesh=mesh, in_specs=placed, out_specs=(thermal, growth, growth), check_vma=False
    )
```

```python
import functools

import jax
import jax.numpy as jnp
from jax import lax
from jax.experimental import pallas as pl
from jax.experimental.pallas import tpu as pltpu
from jax.sharding import PartitionSpec as P

MESH = pl.DeviceIdType.MESH
D = 6
NX, NY, NZ = 16, 32, 128
EX = NX + 2 * D
OY = 8
EY = NY + 2 * OY
PITCH = 3 * D
GR = 16
GX = NX + 4
GY = GR + 16
TINY = 1e-30


def lanes(shape):
    return lax.broadcasted_iota(jnp.int32, shape, 1)


def rows(shape):
    return lax.broadcasted_iota(jnp.int32, shape, 0)


def clip03(heat):
    return jnp.minimum(jnp.maximum(heat, 0.0), 3.0)


def state(heat, base):
    solid = clip03(heat)
    return heat - solid * (2.0 / 3.0), base * (1.0 + solid * (1.0 / 6.0))


def face(temp, cond, temp_next, cond_next):
    total = jnp.maximum(cond + cond_next, TINY)
    return (cond * cond_next) * pltpu.reciprocal(total, approx=True) * (temp_next - temp)


def roll(value, amount, axis):
    return pltpu.roll(value, amount % value.shape[axis], axis)


def shifted(value, amount, axis):
    return roll(value, amount, value.ndim - 2 + axis)


def substep(src, dst, base, step, finish=None):
    first, count = step, EX - 2 * step
    lane_end = lanes((EY, NZ)) == NZ - 1
    before_t, before_k = state(src[first - 1], base[first - 1])
    here_t, here_k = state(src[first], base[first])
    into = face(before_t, before_k, here_t, here_k)

    def slab(x, carry):
        here_t, here_k, into = carry
        next_t, next_k = state(src[x + 1], base[x + 1])
        out_of = face(here_t, here_k, next_t, next_k)
        along_y = face(here_t, here_k, roll(here_t, -1, 0), roll(here_k, -1, 0))
        along_z = face(here_t, here_k, roll(here_t, -1, 1), roll(here_k, -1, 1))
        along_z = jnp.where(lane_end, 0.0, along_z)
        total = (out_of - into) + (along_y - roll(along_y, 1, 0)) + (along_z - roll(along_z, 1, 1))
        heat = src[x] + 0.2 * total
        if finish is None:
            dst[x] = heat
        else:
            finish(x, here_t, heat)
        return next_t, next_k, out_of

    chunk = count // 2

    def several(i, carry):
        for j in range(chunk):
            carry = slab(first + chunk * i + j, carry)
        return carry

    lax.fori_loop(0, 2, several, (here_t, here_k, into))


def last_rows(before, history, base, first):
    near, own = pl.ds(first, 8), pl.ds(D, NX)
    heat = before[pl.ds(D - 1, NX + 2), near]
    temp, cond = state(heat, base[pl.ds(D - 1, NX + 2), near])
    across = face(temp[:-1], cond[:-1], temp[1:], cond[1:])
    temp, cond = temp[1:-1], cond[1:-1]
    lane_end = lax.broadcasted_iota(jnp.int32, temp.shape, 2) == NZ - 1
    along_y = face(temp, cond, roll(temp, -1, 1), roll(cond, -1, 1))
    along_z = face(temp, cond, roll(temp, -1, 2), roll(cond, -1, 2))
    along_z = jnp.where(lane_end, 0.0, along_z)
    total = (
        (across[1:] - across[:-1])
        + (along_y - roll(along_y, 1, 1))
        + (along_z - roll(along_z, 1, 2))
    )
    earlier = [history[s, own, near] for s in range(1, 6)]
    return outcome(earlier, temp, heat[1:-1] + 0.2 * total)[1]


def strip_substep(heat, base, step):
    temp, cond = state(heat, base)
    across = face(temp[:-1], cond[:-1], temp[1:], cond[1:])
    temp, cond = temp[1:-1], cond[1:-1]
    row = lax.broadcasted_iota(jnp.int32, temp.shape, 1)

    def up(v):
        turned = roll(v, -1, 1)
        return jnp.where(row == 7, roll(turned, -PITCH, 2), turned)

    def down(v):
        turned = roll(v, 1, 1)
        return jnp.where(row == 0, roll(turned, PITCH, 2), turned)

    along_y = face(temp, cond, up(temp), up(cond))
    along_z = face(temp, cond, roll(temp, -1, 2), roll(cond, -1, 2))
    total = (across[1:] - across[:-1]) + (along_y - down(along_y)) + (along_z - roll(along_z, 1, 2))
    return heat[1:-1] + 0.2 * total, temp


def outcome(earlier, temp_before, heat):
    solid = clip03(heat)
    temp = heat - solid * (2.0 / 3.0)
    liquid = solid
    for past in earlier:
        liquid = liquid + clip03(past)
    cooling = (temp_before - temp) * 10.0
    under = jnp.maximum(cooling, 0.0) * (0.5 + liquid * (0.1 / 3.0))
    return temp, under * under


def shift_z(low, high):
    lane = lanes(low.shape)
    low_down, high_down = roll(low, 1, 1), roll(high, 1, 1)
    low_up, high_up = roll(low, -1, 1), roll(high, -1, 1)
    zero = jnp.zeros_like(low)
    down = (jnp.where(lane == 0, zero, low_down), jnp.where(lane == 0, low_down, high_down))
    up = (jnp.where(lane == NZ - 1, high_up, low_up), jnp.where(lane == NZ - 1, zero, high_up))
    return down, up


def pick(ref, x, first, count, codes):
    here = (ref[0, x, pl.ds(first, count)], ref[1, x, pl.ds(first, count)])
    down, up = shift_z(*here)
    picked = []
    for half in range(2):
        code = codes[half]
        views = (
            ref[half, x - 1, pl.ds(first, count)],
            ref[half, x + 1, pl.ds(first, count)],
            ref[half, x, pl.ds(first - 1, count)],
            ref[half, x, pl.ds(first + 1, count)],
            down[half],
            up[half],
        )
        value = here[half]
        for number, view in enumerate(views):
            value = jnp.where(code == number + 1, view, value)
        picked.append(value)
    return picked


def loop(start, stop, unroll, step):
    assert (stop - start) % unroll == 0

    def several(i, _):
        for j in range(unroll):
            step(start + unroll * i + j)
        return 0

    lax.fori_loop(0, (stop - start) // unroll, several, 0)


def reach_rows(turns):
    cos_a, sin_a = jnp.cos(turns[0:1]), jnp.sin(turns[0:1])
    cos_b, sin_b = jnp.cos(turns[1:2]), jnp.sin(turns[1:2])
    cos_c, sin_c = jnp.cos(turns[2:3]), jnp.sin(turns[2:3])
    row_x = (
        jnp.abs(cos_a * cos_c - sin_a * sin_c * cos_b)
        + jnp.abs(-cos_a * sin_c - sin_a * cos_c * cos_b)
        + jnp.abs(sin_a * sin_b)
    )
    row_y = (
        jnp.abs(sin_a * cos_c + cos_a * sin_c * cos_b)
        + jnp.abs(-sin_a * sin_c + cos_a * cos_c * cos_b)
        + jnp.abs(-cos_a * sin_b)
    )
    row_z = jnp.abs(sin_c * sin_b) + jnp.abs(cos_c * sin_b) + jnp.abs(cos_b)
    return row_x, row_y, row_z


def lookup(tables, side, code):
    pose = side & 63
    axis = jnp.maximum(code - 1, 0) >> 1
    parts = []
    for tile in range(side.shape[0] // 8):
        cut = slice(8 * tile, 8 * tile + 8)
        index = pose[cut] + ((axis[cut] & 1) << 6)
        xy = jnp.take_along_axis(tables[0], index, axis=1, mode="promise_in_bounds")
        z = jnp.take_along_axis(tables[1], index, axis=1, mode="promise_in_bounds")
        parts.append(jnp.where(code[cut] > 0, jnp.where(axis[cut] == 2, z, xy), 0.0))
    return jnp.concatenate(parts, axis=0)


def kernel(
    kelvin_hbm, conductance_hbm, melted_hbm, germ_hbm, nucleus_hbm, pose_hbm, captured_hbm,
    roster_hbm, turns_hbm,
    temp_out, env_out, grain_out,
    kelvin, conductance, melted, germ, nucleus, pose, captured, roster, turns, load_sem,
    temp_own, env_own, grain_own, save_sem,
    bricks, history, strip_h, strip_b, strip_out, strip_in, speed,
    far, strip_t, strip_s, lab, lab1, reach1, reach2, gspeed, grown1, env1,
    heat_send, heat_recv, strip_send, strip_recv,
    speed_send, speed_recv_a, speed_recv_b, local_sem, lab_send, lab_recv,
):
    gx, gy, gz = (lax.axis_index(a) for a in ("gx", "gy", "gz"))
    ngx, ngy = lax.axis_size("gx"), lax.axis_size("gy")

    def at(dx, dy, z):
        return (lax.rem(gx + dx + ngx, ngx), lax.rem(gy + dy + ngy, ngy), z)

    other = 1 - gz
    cross = 2 * gz - 1
    xy = [(0, -1), (0, 1), (-1, -1), (1, 1), (-1, 1), (1, -1), (-1, 0), (1, 0)]
    greeted = [at(dx, dy, gz) for dx, dy in xy]
    greeted += [at(dx, 0, other) for dx in (-1, 0, 1)]
    greeted += [at(dx, cross, other) for dx in (-1, 0, 1)]
    barrier = pltpu.get_barrier_semaphore()
    for device in greeted:
        pl.semaphore_signal(barrier, inc=1, device_id=device, device_id_type=MESH)

    loads = [
        pltpu.make_async_copy(src, dst, load_sem.at[i])
        for i, (src, dst) in enumerate((
            (kelvin_hbm, kelvin), (melted_hbm, melted), (conductance_hbm, conductance),
            (germ_hbm, germ), (nucleus_hbm, nucleus), (pose_hbm, pose),
            (captured_hbm, captured), (roster_hbm, roster), (turns_hbm, turns),
        ))
    ]
    for load in loads:
        load.start()

    def send(src, dst, send_sem, recv_sem, device):
        copy = pltpu.make_async_remote_copy(
            src_ref=src, dst_ref=dst, send_sem=send_sem, recv_sem=recv_sem,
            device_id=device, device_id_type=MESH,
        )
        copy.start()
        return copy

    own_rows = pl.ds(OY, NY)

    def opening(x):
        melt = melted[x].astype(jnp.float32)
        start = kelvin[x] + 1.5 * melt
        bricks[0, D + x, own_rows] = start + 2.0 * jnp.clip(start, 0.0, 1.0)
        bricks[1, D + x, own_rows] = conductance[x] * (0.25 + 0.75 * melt)

    for load in loads[:3]:
        load.wait()
    loop(0, NX, 4, opening)

    for load in loads[3:]:
        load.wait()
    tiles = [roster[0, 0, i] for i in range(8)]

    def seeds(x):
        tile = x // 2
        active = tiles[0] == tile
        for number in tiles[1:]:
            active = jnp.logical_or(active, number == tile)
        for half in range(2):
            cut = pl.ds(half * NZ, NZ)
            label = germ[x, :, cut] * (nucleus[x, :, cut] * 64 + pose[x, :, cut])
            lab[0, half, 2 + x, pl.ds(8, GR)] = label
            for g in range(2):
                lab[1 + g, half, 2 + x, pl.ds(8, GR)] = jnp.where(
                    active, captured[g, x, :, cut], -1
                )

    loop(0, NX, 2, seeds)

    pl.semaphore_wait(barrier, len(greeted))

    copies = []
    for i, (dx, dy) in enumerate(xy):
        deep = D if dx == 0 or dy == 0 else D - 1
        src_x = {-1: (D, deep), 0: (D, NX), 1: (D + NX - deep, deep)}[dx]
        dst_x = {-1: D + NX, 0: D, 1: D - deep}[dx]
        src_y = {-1: (OY, deep), 0: (OY, NY), 1: (OY + NY - deep, deep)}[dy]
        dst_y = {-1: OY + NY, 0: OY, 1: OY - deep}[dy]
        copies.append(send(
            bricks.at[:, pl.ds(*src_x), pl.ds(*src_y)],
            bricks.at[:, pl.ds(dst_x, src_x[1]), pl.ds(dst_y, src_y[1])],
            heat_send.at[i], heat_recv.at[i], at(dx, dy, gz),
        ))

    row_x, row_y, row_z = reach_rows(turns[...])
    tables = [
        jnp.broadcast_to(jnp.concatenate(pair, axis=1), (8, NZ))
        for pair in ((row_x, row_y), (row_z, row_z))
    ]

    lane8 = lanes((8, NZ))
    slot = lane8
    for tile in range(1, EY // 8):
        slot = jnp.where(lane8 >= tile * PITCH, lane8 - tile * PITCH, slot)
    in_use = lane8 < PITCH * (EY // 8)
    own_slot = (slot >= D * gz) & (slot < D * gz + 2 * D)
    halo_slot = jnp.logical_not(own_slot) & in_use
    turn = D * (1 - 2 * gz)

    def pack(x, ref, values, strip):
        for tile, value in values:
            moved = pltpu.roll(value, (PITCH * tile + 2 * D - D * gz) % NZ, 1)
            mine = own_slot & (lane8 >= tile * PITCH) & (lane8 < (tile + 1) * PITCH)
            strip = jnp.where(mine, moved, strip)
        ref[x] = strip
        return strip

    empty = jnp.zeros((8, NZ), jnp.float32)
    inside = range(OY // 8, (OY + NY) // 8)

    def pack_own(x):
        for part, ref in enumerate((strip_h, strip_b)):
            pack(x, ref, [(tile, bricks[part, x, pl.ds(8 * tile, 8)]) for tile in inside], empty)

    loop(D, D + NX, 4, pack_own)

    for copy in copies:
        copy.wait()

    def pack_halo(x, tiles, begun):
        outside_x = ((x < D) & (gx == 0)) | ((x >= D + NX) & (gx == ngx - 1))
        bases = []
        for tile in tiles:
            outside = outside_x
            if tile == 0:
                outside = outside | (gy == 0)
            if tile == EY // 8 - 1:
                outside = outside | (gy == ngy - 1)
            put = pl.ds(8 * tile, 8)
            base = jnp.where(outside, 0.0, bricks[1, x, put])
            bricks[1, x, put] = base
            bases.append((tile, base))
        heats = [(tile, bricks[0, x, pl.ds(8 * tile, 8)]) for tile in tiles]
        heat = pack(x, strip_h, heats, strip_h[x] if begun else empty)
        base = pack(x, strip_b, bases, strip_b[x] if begun else empty)
        strip_out[x] = jnp.where(halo_slot, pltpu.roll(base, (turn + NZ) % NZ, 1), heat)

    every = range(EY // 8)
    loop(0, D, 3, lambda x: pack_halo(x, every, False))
    loop(D + NX, EX, 3, lambda x: pack_halo(x, every, False))
    loop(D, D + NX, 4, lambda x: pack_halo(x, (0, EY // 8 - 1), True))
    strip_copy = send(
        strip_out, strip_in, strip_send, strip_recv, at(0, 0, other)
    )

    lab_copies = []
    for i, (dx, dg) in enumerate(xy):
        deep = 2 if dx == 0 or dg == 0 else 1
        src_x = {-1: (2, deep), 0: (2, NX), 1: (2 + NX - deep, deep)}[dx]
        dst_x = {-1: 2 + NX, 0: 2, 1: 2 - deep}[dx]
        src_y = {-1: (8, deep), 0: (8, GR), 1: (8 + GR - deep, deep)}[dg]
        dst_y = {-1: 8 + GR, 0: 8, 1: 8 - deep}[dg]
        if dg == 0:
            device = at(dx, 0, gz)
        elif dg == 1:
            device = at(dx, gz, other)
        else:
            device = at(dx, gz - 1, other)
        lab_copies.append(send(
            lab.at[pl.ds(0, 2), :, pl.ds(*src_x), pl.ds(*src_y)],
            lab.at[pl.ds(0, 2), :, pl.ds(dst_x, src_x[1]), pl.ds(dst_y, src_y[1])],
            lab_send.at[i], lab_recv.at[i], device,
        ))

    for step in range(1, 6):
        before = bricks.at[0] if step == 1 else history.at[step - 1]
        substep(before, history.at[step], bricks.at[1], step)

    strip_copy.wait()

    def unpack(x):
        got = strip_in[x]
        strip_h[x] = jnp.where(halo_slot, pltpu.roll(got, (turn + NZ) % NZ, 1), strip_h[x])
        strip_b[x] = jnp.where(halo_slot, pltpu.roll(got, (2 * turn + NZ) % NZ, 1), strip_b[x])

    loop(0, EX, 14, unpack)
    heat = strip_h[...]
    earlier = []
    for step in range(1, 7):
        heat, temp_before = strip_substep(heat, strip_b[pl.ds(step - 1, EX + 2 - 2 * step)], step)
        if step < 6:
            earlier.append(heat[D - step : D - step + NX])
    strip_t[...], strip_s[...] = outcome(earlier, temp_before, heat)

    near = jnp.where(gz == 0, lane8 - (NZ - D), D - 1 - lane8) >= 0

    speed_copies = []

    def tell(dx, dy, z, number, recv_sem):
        if dy == 0:
            deep_x = 2
            src_y, dst_y, count_y = 14 * z, 8 - 2 * z, 18
        else:
            deep_x = 1
            count_y = 2 if dx == 0 else 1
            src_y = 2 - count_y if dy == 1 else 0
            dst_y = 8 - count_y if dy == 1 else 8 + GR
        src_x = {-1: (0, deep_x), 0: (0, NX), 1: (NX - deep_x, deep_x)}[dx]
        dst_x = {-1: 2 + NX, 0: 2, 1: 2 - deep_x}[dx]
        source = speed if dy == 0 else far.at[(1 - dy) // 2]
        speed_copies.append(send(
            source.at[pl.ds(*src_x), pl.ds(src_y, count_y)],
            gspeed.at[gz, pl.ds(dst_x, src_x[1]), pl.ds(dst_y, count_y)],
            speed_send.at[number], recv_sem, at(dx, dy, z),
        ))

    turned = [
        pltpu.roll(strip_s[...], (NZ - 2 * D + D * gz - PITCH * (tile + 1) + NZ) % NZ, 2)
        for tile in (NY // 8 - 1, 0)
    ]
    near_all = jnp.broadcast_to(near[None], (NX, 8, NZ))
    upper = last_rows(history.at[5], history, bricks.at[1], OY + NY - 7)
    upper = jnp.where(near_all, turned[0], roll(upper, 1, 1))
    lower = last_rows(history.at[5], history, bricks.at[1], OY - 1)
    lower = jnp.where(near_all, turned[1], roll(lower, -1, 1))
    far[0, :, pl.ds(0, 2)] = upper[:, 6:8]
    far[1, :, pl.ds(0, 2)] = lower[:, 0:2]
    for dx in (0, -1, 1):
        for dy, z in ((1, 0), (-1, 1)):
            tell(dx, dy, z, len(speed_copies), speed_recv_b.at[dx + 1, gz])

    def brick_end(x, temp_before, heat):
        temp, fast = outcome([history[s, x] for s in range(1, 6)], temp_before, heat)
        for tile in range(NY // 8):
            cut = slice(OY + 8 * tile, OY + 8 * tile + 8)
            back = (NZ - 2 * D + D * gz - PITCH * (tile + 1) + NZ) % NZ
            put = pl.ds(8 * tile, 8)
            temp_own[x - D, put] = jnp.where(
                near, pltpu.roll(strip_t[x - D], back, 1), temp[cut]
            )
            speed[x - D, put] = jnp.where(
                near, pltpu.roll(strip_s[x - D], back, 1), fast[cut]
            )

    substep(history.at[5], None, bricks.at[1], 6, brick_end)
    temp_save = pltpu.make_async_copy(temp_own, temp_out, save_sem.at[0])
    temp_save.start()

    for dx in (-1, 1):
        for z in range(2):
            tell(dx, 0, z, len(speed_copies), speed_recv_a.at[dx + 1, gz])
    tell(0, 0, other, len(speed_copies), speed_recv_a.at[1, gz])
    keep = pltpu.make_async_copy(
        speed.at[:, pl.ds(14 * gz, 18)],
        gspeed.at[gz, pl.ds(2, NX), pl.ds(8 - 2 * gz, 18)],
        local_sem,
    )
    keep.start()

    for copy in lab_copies:
        copy.wait()
    row_g = rows((GY, NZ))
    outside_g = ((row_g < 8) & (gy + gz == 0)) | (
        (row_g >= 8 + GR) & (gy + gz == ngy)
    )

    def border(x):
        outside = outside_g | ((x < 2) & (gx == 0)) | ((x >= 2 + NX) & (gx == ngx - 1))
        for half in range(2):
            lab[0, half, x] = jnp.where(outside, 0, lab[0, half, x])
            lab[1, half, x] = jnp.where(outside, -1, lab[1, half, x])

    loop(0, GX, 2, border)
    wide = pl.ds(7, 24)
    own = pl.ds(8, GR)

    def first_labels(x):
        codes = [lab[1, half, x, wide] for half in range(2)]
        sides = pick(lab.at[0], x, 7, 24, codes)
        for half in range(2):
            lab1[half, x, wide] = sides[half]
            reach1[half, x, wide] = lookup(tables, sides[half], codes[half])

    loop(1, GX - 1, 3, first_labels)

    def second_labels(x):
        codes = [lab[2, half, x, own] for half in range(2)]
        sides = pick(lab1, x, 8, GR, codes)
        for half in range(2):
            grain_own[x - 2, :, pl.ds(half * NZ, NZ)] = sides[half] >> 6
            reach2[half, x, own] = lookup(tables, sides[half], codes[half])

    loop(2, GX - 2, 4, second_labels)
    grain_save = pltpu.make_async_copy(grain_own, grain_out, save_sem.at[1])
    grain_save.start()

    for copy in speed_copies:
        copy.wait_send()
    keep.wait()

    def heard(count_x, count_y, recv_sem):
        pltpu.make_async_remote_copy(
            src_ref=speed.at[pl.ds(0, count_x), pl.ds(0, count_y)],
            dst_ref=gspeed.at[0, pl.ds(0, count_x), pl.ds(0, count_y)],
            send_sem=speed_send.at[0], recv_sem=recv_sem,
            device_id=at(0, 0, other), device_id_type=MESH,
        ).wait_recv()

    for z in range(2):
        for dx in (-1, 1):
            heard(2, 18, speed_recv_a.at[dx + 1, z])
            heard(1, 1, speed_recv_b.at[dx + 1, z])
        heard(NX, 2, speed_recv_b.at[1, z])
    heard(NX, 18, speed_recv_a.at[1, other])

    def first_growth(x):
        codes = [lab[1, half, x, wide] for half in range(2)]
        sides = pick(gspeed, x, 7, 24, codes)
        for half in range(2):
            solid = lab1[half, x, wide] > 0
            caught = jnp.maximum(sides[half] - reach1[half, x, wide], 0.0)
            envelope = jnp.where(solid & (codes[half] >= 0), caught, 0.0)
            env1[half, x, wide] = envelope
            grown1[half, x, wide] = envelope + jnp.where(solid, gspeed[half, x, wide], 0.0)

    loop(1, GX - 1, 3, first_growth)

    def second_growth(x):
        codes = [lab[2, half, x, own] for half in range(2)]
        sides = pick(grown1, x, 8, GR, codes)
        for half in range(2):
            caught = jnp.maximum(sides[half] - reach2[half, x, own], 0.0)
            env_own[x - 2, :, pl.ds(half * NZ, NZ)] = jnp.where(
                codes[half] < 0, env1[half, x, own], caught
            )

    saves = [temp_save, grain_save]
    for part in range(2):
        cut = pl.ds(NX // 2 * part, NX // 2)
        loop(2 + NX // 2 * part, 2 + NX // 2 * (part + 1), 4, second_growth)
        saves.append(pltpu.make_async_copy(env_own.at[cut], env_out.at[cut], save_sem.at[2 + part]))
        saves[-1].start()
    for save in saves:
        save.wait()


def handing_on(*refs):
    sources, targets, held, sems = refs[:3], refs[3:6], refs[6:9], refs[9]
    fetches = [pltpu.make_async_copy(sources[i], held[i], sems.at[0, i]) for i in range(3)]
    stores = [pltpu.make_async_copy(held[i], targets[i], sems.at[1, i]) for i in range(3)]
    for fetch in fetches:
        fetch.start()
    for fetch, store in zip(fetches, stores):
        fetch.wait()
        store.start()
    for store in stores:
        store.wait()


def body(*args):
    hbm = pl.BlockSpec(memory_space=pltpu.HBM)
    f32, i32 = jnp.float32, jnp.int32
    dma = pltpu.SemaphoreType.DMA
    growth = (2, GX, GY, NZ)
    results = (
        jax.ShapeDtypeStruct((NX, NY, NZ), f32),
        jax.ShapeDtypeStruct((NX, GR, 2 * NZ), f32),
        jax.ShapeDtypeStruct((NX, GR, 2 * NZ), i32),
    )
    made = pl.pallas_call(
        kernel,
        out_shape=results,
        in_specs=[hbm] * 9,
        out_specs=(hbm, hbm, hbm),
        scratch_shapes=[
            pltpu.VMEM((NX, NY, NZ), f32),
            pltpu.VMEM((NX, NY, NZ), f32),
            pltpu.VMEM((NX, NY, NZ), i32),
            pltpu.VMEM((NX, GR, 2 * NZ), i32),
            pltpu.VMEM((NX, GR, 2 * NZ), i32),
            pltpu.VMEM((NX, GR, 2 * NZ), i32),
            pltpu.VMEM((2, NX, GR, 2 * NZ), i32),
            pltpu.SMEM((1, 1, 8), i32),
            pltpu.VMEM((3, 64), f32),
            dma((9,)),
            pltpu.VMEM((NX, NY, NZ), f32),
            pltpu.VMEM((NX, GR, 2 * NZ), f32),
            pltpu.VMEM((NX, GR, 2 * NZ), i32),
            dma((4,)),
            pltpu.VMEM((2, EX, EY, NZ), f32),
            pltpu.VMEM((6, EX, EY, NZ), f32),
            pltpu.VMEM((EX, 8, NZ), f32),
            pltpu.VMEM((EX, 8, NZ), f32),
            pltpu.VMEM((EX, 8, NZ), f32),
            pltpu.VMEM((EX, 8, NZ), f32),
            pltpu.VMEM((NX, NY, NZ), f32),
            pltpu.VMEM((2, NX, 8, NZ), f32),
            pltpu.VMEM((NX, 8, NZ), f32),
            pltpu.VMEM((NX, 8, NZ), f32),
            pltpu.VMEM((3,) + growth, i32),
            pltpu.VMEM(growth, i32),
            pltpu.VMEM(growth, f32),
            pltpu.VMEM(growth, f32),
            pltpu.VMEM(growth, f32),
            pltpu.VMEM(growth, f32),
            pltpu.VMEM(growth, f32),
            dma((8,)), dma((8,)), dma, dma,
            dma((14,)), dma((3, 2)), dma((3, 2)), dma, dma((8,)), dma((8,)),
        ],
        compiler_params=pltpu.CompilerParams(
            collective_id=0, has_side_effects=True, vmem_limit_bytes=62 << 20
        ),
    )(*args)
    return pl.pallas_call(
        handing_on,
        out_shape=results,
        in_specs=[hbm] * 3,
        out_specs=(hbm, hbm, hbm),
        scratch_shapes=[pltpu.VMEM(r.shape, r.dtype) for r in results] + [dma((2, 3))],
        compiler_params=pltpu.CompilerParams(vmem_limit_bytes=62 << 20),
    )(*made)


def solution(mesh):
    thermal = P("gx", "gy", "gz")
    growth = P("gx", ("gy", "gz"), None)
    placed = (
        thermal, thermal, thermal, growth, growth, growth,
        P(None, "gx", ("gy", "gz"), None), growth, P(),
    )
    return jax.shard_map(
        body, mesh=mesh, in_specs=placed, out_specs=(thermal, growth, growth), check_vma=False
    )
```

```python
import functools

import jax
import jax.numpy as jnp
from jax import lax
from jax.experimental import pallas as pl
from jax.experimental.pallas import tpu as pltpu
from jax.sharding import PartitionSpec as P

MESH = pl.DeviceIdType.MESH
D = 6
NX, NY, NZ = 16, 32, 128
EX = NX + 2 * D
OY = 8
EY = NY + 2 * OY
PITCH = 3 * D
GR = 16
GX = NX + 4
GY = GR + 16
TINY = 1e-30


def lanes(shape):
    return lax.broadcasted_iota(jnp.int32, shape, 1)


def rows(shape):
    return lax.broadcasted_iota(jnp.int32, shape, 0)


def clip03(heat):
    return jnp.minimum(jnp.maximum(heat, 0.0), 3.0)


def state(heat, base):
    solid = clip03(heat)
    return heat - solid * (2.0 / 3.0), base * (1.0 + solid * (1.0 / 6.0))


def face(temp, cond, temp_next, cond_next):
    total = jnp.maximum(cond + cond_next, TINY)
    return (cond * cond_next) * pltpu.reciprocal(total, approx=True) * (temp_next - temp)


def roll(value, amount, axis):
    return pltpu.roll(value, amount % value.shape[axis], axis)


def shifted(value, amount, axis):
    return roll(value, amount, value.ndim - 2 + axis)


def substep(src, dst, base, step, finish=None):
    first, count = step, EX - 2 * step
    lane_end = lanes((EY, NZ)) == NZ - 1
    before_t, before_k = state(src[first - 1], base[first - 1])
    here_t, here_k = state(src[first], base[first])
    into = face(before_t, before_k, here_t, here_k)

    def slab(x, carry):
        here_t, here_k, into = carry
        next_t, next_k = state(src[x + 1], base[x + 1])
        out_of = face(here_t, here_k, next_t, next_k)
        along_y = face(here_t, here_k, roll(here_t, -1, 0), roll(here_k, -1, 0))
        along_z = face(here_t, here_k, roll(here_t, -1, 1), roll(here_k, -1, 1))
        along_z = jnp.where(lane_end, 0.0, along_z)
        total = (out_of - into) + (along_y - roll(along_y, 1, 0)) + (along_z - roll(along_z, 1, 1))
        heat = src[x] + 0.2 * total
        if finish is None:
            dst[x] = heat
        else:
            finish(x, here_t, heat)
        return next_t, next_k, out_of

    chunk = count // 2

    def several(i, carry):
        for j in range(chunk):
            carry = slab(first + chunk * i + j, carry)
        return carry

    lax.fori_loop(0, 2, several, (here_t, here_k, into))


def last_rows(before, history, base, first):
    near, own = pl.ds(first, 8), pl.ds(D, NX)
    heat = before[pl.ds(D - 1, NX + 2), near]
    temp, cond = state(heat, base[pl.ds(D - 1, NX + 2), near])
    across = face(temp[:-1], cond[:-1], temp[1:], cond[1:])
    temp, cond = temp[1:-1], cond[1:-1]
    lane_end = lax.broadcasted_iota(jnp.int32, temp.shape, 2) == NZ - 1
    along_y = face(temp, cond, roll(temp, -1, 1), roll(cond, -1, 1))
    along_z = face(temp, cond, roll(temp, -1, 2), roll(cond, -1, 2))
    along_z = jnp.where(lane_end, 0.0, along_z)
    total = (
        (across[1:] - across[:-1])
        + (along_y - roll(along_y, 1, 1))
        + (along_z - roll(along_z, 1, 2))
    )
    earlier = [history[s, own, near] for s in range(1, 6)]
    return outcome(earlier, temp, heat[1:-1] + 0.2 * total)[1]


def strip_substep(heat, base, step):
    temp, cond = state(heat, base)
    across = face(temp[:-1], cond[:-1], temp[1:], cond[1:])
    temp, cond = temp[1:-1], cond[1:-1]
    row = lax.broadcasted_iota(jnp.int32, temp.shape, 1)

    def up(v):
        turned = roll(v, -1, 1)
        return jnp.where(row == 7, roll(turned, -PITCH, 2), turned)

    def down(v):
        turned = roll(v, 1, 1)
        return jnp.where(row == 0, roll(turned, PITCH, 2), turned)

    along_y = face(temp, cond, up(temp), up(cond))
    along_z = face(temp, cond, roll(temp, -1, 2), roll(cond, -1, 2))
    total = (across[1:] - across[:-1]) + (along_y - down(along_y)) + (along_z - roll(along_z, 1, 2))
    return heat[1:-1] + 0.2 * total, temp


def outcome(earlier, temp_before, heat):
    solid = clip03(heat)
    temp = heat - solid * (2.0 / 3.0)
    liquid = solid
    for past in earlier:
        liquid = liquid + clip03(past)
    cooling = (temp_before - temp) * 10.0
    under = jnp.maximum(cooling, 0.0) * (0.5 + liquid * (0.1 / 3.0))
    return temp, under * under


def shift_z(low, high):
    lane = lanes(low.shape)
    low_down, high_down = roll(low, 1, 1), roll(high, 1, 1)
    low_up, high_up = roll(low, -1, 1), roll(high, -1, 1)
    zero = jnp.zeros_like(low)
    down = (jnp.where(lane == 0, zero, low_down), jnp.where(lane == 0, low_down, high_down))
    up = (jnp.where(lane == NZ - 1, high_up, low_up), jnp.where(lane == NZ - 1, zero, high_up))
    return down, up


def pick(ref, x, first, count, codes):
    here = (ref[0, x, pl.ds(first, count)], ref[1, x, pl.ds(first, count)])
    down, up = shift_z(*here)
    picked = []
    for half in range(2):
        code = codes[half]
        views = (
            ref[half, x - 1, pl.ds(first, count)],
            ref[half, x + 1, pl.ds(first, count)],
            ref[half, x, pl.ds(first - 1, count)],
            ref[half, x, pl.ds(first + 1, count)],
            down[half],
            up[half],
        )
        value = here[half]
        for number, view in enumerate(views):
            value = jnp.where(code == number + 1, view, value)
        picked.append(value)
    return picked


def loop(start, stop, unroll, step):
    assert (stop - start) % unroll == 0

    def several(i, _):
        for j in range(unroll):
            step(start + unroll * i + j)
        return 0

    lax.fori_loop(0, (stop - start) // unroll, several, 0)


def reach_rows(turns):
    cos_a, sin_a = jnp.cos(turns[0:1]), jnp.sin(turns[0:1])
    cos_b, sin_b = jnp.cos(turns[1:2]), jnp.sin(turns[1:2])
    cos_c, sin_c = jnp.cos(turns[2:3]), jnp.sin(turns[2:3])
    row_x = (
        jnp.abs(cos_a * cos_c - sin_a * sin_c * cos_b)
        + jnp.abs(-cos_a * sin_c - sin_a * cos_c * cos_b)
        + jnp.abs(sin_a * sin_b)
    )
    row_y = (
        jnp.abs(sin_a * cos_c + cos_a * sin_c * cos_b)
        + jnp.abs(-sin_a * sin_c + cos_a * cos_c * cos_b)
        + jnp.abs(-cos_a * sin_b)
    )
    row_z = jnp.abs(sin_c * sin_b) + jnp.abs(cos_c * sin_b) + jnp.abs(cos_b)
    return row_x, row_y, row_z


def lookup(tables, side, code):
    pose = side & 63
    axis = jnp.maximum(code - 1, 0) >> 1
    parts = []
    for tile in range(side.shape[0] // 8):
        cut = slice(8 * tile, 8 * tile + 8)
        index = pose[cut] + ((axis[cut] & 1) << 6)
        xy = jnp.take_along_axis(tables[0], index, axis=1, mode="promise_in_bounds")
        z = jnp.take_along_axis(tables[1], index, axis=1, mode="promise_in_bounds")
        parts.append(jnp.where(code[cut] > 0, jnp.where(axis[cut] == 2, z, xy), 0.0))
    return jnp.concatenate(parts, axis=0)


def kernel(
    kelvin_hbm, conductance_hbm, melted_hbm, germ_hbm, nucleus_hbm, pose_hbm, captured_hbm,
    roster_hbm, turns_hbm,
    temp_out, env_out, grain_out,
    kelvin, conductance, melted, germ, nucleus, pose, captured, roster, turns, load_sem,
    temp_own, env_own, grain_own, save_sem,
    bricks, history, strip_h, strip_b, strip_out, strip_in, speed,
    far, strip_t, strip_s, lab, lab1, reach1, reach2, gspeed, grown1, env1,
    heat_send, heat_recv, strip_send, strip_recv,
    speed_send, speed_recv_a, speed_recv_b, local_sem, lab_send, lab_recv,
):
    gx, gy, gz = (lax.axis_index(a) for a in ("gx", "gy", "gz"))
    ngx, ngy = lax.axis_size("gx"), lax.axis_size("gy")

    def at(dx, dy, z):
        return (lax.rem(gx + dx + ngx, ngx), lax.rem(gy + dy + ngy, ngy), z)

    other = 1 - gz
    cross = 2 * gz - 1
    xy = [(0, -1), (0, 1), (-1, -1), (1, 1), (-1, 1), (1, -1), (-1, 0), (1, 0)]
    greeted = [at(dx, dy, gz) for dx, dy in xy]
    greeted += [at(dx, 0, other) for dx in (-1, 0, 1)]
    greeted += [at(dx, cross, other) for dx in (-1, 0, 1)]
    barrier = pltpu.get_barrier_semaphore()
    for device in greeted:
        pl.semaphore_signal(barrier, inc=1, device_id=device, device_id_type=MESH)

    loads = [
        pltpu.make_async_copy(src, dst, load_sem.at[i])
        for i, (src, dst) in enumerate((
            (kelvin_hbm, kelvin), (melted_hbm, melted), (conductance_hbm, conductance),
            (germ_hbm, germ), (nucleus_hbm, nucleus), (pose_hbm, pose),
            (captured_hbm, captured), (roster_hbm, roster), (turns_hbm, turns),
        ))
    ]
    for load in loads:
        load.start()

    def send(src, dst, send_sem, recv_sem, device):
        copy = pltpu.make_async_remote_copy(
            src_ref=src, dst_ref=dst, send_sem=send_sem, recv_sem=recv_sem,
            device_id=device, device_id_type=MESH,
        )
        copy.start()
        return copy

    own_rows = pl.ds(OY, NY)

    def opening(x):
        melt = melted[x].astype(jnp.float32)
        start = kelvin[x] + 1.5 * melt
        bricks[0, D + x, own_rows] = start + 2.0 * jnp.clip(start, 0.0, 1.0)
        bricks[1, D + x, own_rows] = conductance[x] * (0.25 + 0.75 * melt)

    for load in loads[:3]:
        load.wait()
    loop(0, NX, 4, opening)

    for load in loads[3:]:
        load.wait()
    tiles = [roster[0, 0, i] for i in range(8)]

    def seeds(x):
        tile = x // 2
        active = tiles[0] == tile
        for number in tiles[1:]:
            active = jnp.logical_or(active, number == tile)
        for half in range(2):
            cut = pl.ds(half * NZ, NZ)
            label = germ[x, :, cut] * (nucleus[x, :, cut] * 64 + pose[x, :, cut])
            lab[0, half, 2 + x, pl.ds(8, GR)] = label
            for g in range(2):
                lab[1 + g, half, 2 + x, pl.ds(8, GR)] = jnp.where(
                    active, captured[g, x, :, cut], -1
                )

    loop(0, NX, 2, seeds)

    pl.semaphore_wait(barrier, len(greeted))

    copies = []
    for i, (dx, dy) in enumerate(xy):
        deep = D if dx == 0 or dy == 0 else D - 1
        src_x = {-1: (D, deep), 0: (D, NX), 1: (D + NX - deep, deep)}[dx]
        dst_x = {-1: D + NX, 0: D, 1: D - deep}[dx]
        src_y = {-1: (OY, deep), 0: (OY, NY), 1: (OY + NY - deep, deep)}[dy]
        dst_y = {-1: OY + NY, 0: OY, 1: OY - deep}[dy]
        copies.append(send(
            bricks.at[:, pl.ds(*src_x), pl.ds(*src_y)],
            bricks.at[:, pl.ds(dst_x, src_x[1]), pl.ds(dst_y, src_y[1])],
            heat_send.at[i], heat_recv.at[i], at(dx, dy, gz),
        ))

    row_x, row_y, row_z = reach_rows(turns[...])
    tables = [
        jnp.broadcast_to(jnp.concatenate(pair, axis=1), (8, NZ))
        for pair in ((row_x, row_y), (row_z, row_z))
    ]

    lane8 = lanes((8, NZ))
    slot = lane8
    for tile in range(1, EY // 8):
        slot = jnp.where(lane8 >= tile * PITCH, lane8 - tile * PITCH, slot)
    in_use = lane8 < PITCH * (EY // 8)
    own_slot = (slot >= D * gz) & (slot < D * gz + 2 * D)
    halo_slot = jnp.logical_not(own_slot) & in_use
    turn = D * (1 - 2 * gz)

    def pack(x, ref, values, strip):
        for tile, value in values:
            moved = pltpu.roll(value, (PITCH * tile + 2 * D - D * gz) % NZ, 1)
            mine = own_slot & (lane8 >= tile * PITCH) & (lane8 < (tile + 1) * PITCH)
            strip = jnp.where(mine, moved, strip)
        ref[x] = strip
        return strip

    empty = jnp.zeros((8, NZ), jnp.float32)
    inside = range(OY // 8, (OY + NY) // 8)

    def pack_own(x):
        for part, ref in enumerate((strip_h, strip_b)):
            pack(x, ref, [(tile, bricks[part, x, pl.ds(8 * tile, 8)]) for tile in inside], empty)

    loop(D, D + NX, 4, pack_own)

    for copy in copies:
        copy.wait()

    def pack_halo(x, tiles, begun):
        outside_x = ((x < D) & (gx == 0)) | ((x >= D + NX) & (gx == ngx - 1))
        bases = []
        for tile in tiles:
            outside = outside_x
            if tile == 0:
                outside = outside | (gy == 0)
            if tile == EY // 8 - 1:
                outside = outside | (gy == ngy - 1)
            put = pl.ds(8 * tile, 8)
            base = jnp.where(outside, 0.0, bricks[1, x, put])
            bricks[1, x, put] = base
            bases.append((tile, base))
        heats = [(tile, bricks[0, x, pl.ds(8 * tile, 8)]) for tile in tiles]
        heat = pack(x, strip_h, heats, strip_h[x] if begun else empty)
        base = pack(x, strip_b, bases, strip_b[x] if begun else empty)
        strip_out[x] = jnp.where(halo_slot, pltpu.roll(base, (turn + NZ) % NZ, 1), heat)

    every = range(EY // 8)
    loop(0, D, 6, lambda x: pack_halo(x, every, False))
    loop(D + NX, EX, 6, lambda x: pack_halo(x, every, False))
    loop(D, D + NX, 8, lambda x: pack_halo(x, (0, EY // 8 - 1), True))
    strip_copy = send(
        strip_out, strip_in, strip_send, strip_recv, at(0, 0, other)
    )

    lab_copies = []
    for i, (dx, dg) in enumerate(xy):
        deep = 2 if dx == 0 or dg == 0 else 1
        src_x = {-1: (2, deep), 0: (2, NX), 1: (2 + NX - deep, deep)}[dx]
        dst_x = {-1: 2 + NX, 0: 2, 1: 2 - deep}[dx]
        src_y = {-1: (8, deep), 0: (8, GR), 1: (8 + GR - deep, deep)}[dg]
        dst_y = {-1: 8 + GR, 0: 8, 1: 8 - deep}[dg]
        if dg == 0:
            device = at(dx, 0, gz)
        elif dg == 1:
            device = at(dx, gz, other)
        else:
            device = at(dx, gz - 1, other)
        lab_copies.append(send(
            lab.at[pl.ds(0, 2), :, pl.ds(*src_x), pl.ds(*src_y)],
            lab.at[pl.ds(0, 2), :, pl.ds(dst_x, src_x[1]), pl.ds(dst_y, src_y[1])],
            lab_send.at[i], lab_recv.at[i], device,
        ))

    for step in range(1, 6):
        before = bricks.at[0] if step == 1 else history.at[step - 1]
        substep(before, history.at[step], bricks.at[1], step)

    strip_copy.wait()

    def unpack(x):
        got = strip_in[x]
        strip_h[x] = jnp.where(halo_slot, pltpu.roll(got, (turn + NZ) % NZ, 1), strip_h[x])
        strip_b[x] = jnp.where(halo_slot, pltpu.roll(got, (2 * turn + NZ) % NZ, 1), strip_b[x])

    loop(0, EX, 14, unpack)
    heat = strip_h[...]
    earlier = []
    for step in range(1, 7):
        heat, temp_before = strip_substep(heat, strip_b[pl.ds(step - 1, EX + 2 - 2 * step)], step)
        if step < 6:
            earlier.append(heat[D - step : D - step + NX])
    strip_t[...], strip_s[...] = outcome(earlier, temp_before, heat)

    near = jnp.where(gz == 0, lane8 - (NZ - D), D - 1 - lane8) >= 0

    speed_copies = []

    def tell(dx, dy, z, number, recv_sem):
        if dy == 0:
            deep_x = 2
            src_y, dst_y, count_y = 14 * z, 8 - 2 * z, 18
        else:
            deep_x = 1
            count_y = 2 if dx == 0 else 1
            src_y = 2 - count_y if dy == 1 else 0
            dst_y = 8 - count_y if dy == 1 else 8 + GR
        src_x = {-1: (0, deep_x), 0: (0, NX), 1: (NX - deep_x, deep_x)}[dx]
        dst_x = {-1: 2 + NX, 0: 2, 1: 2 - deep_x}[dx]
        source = speed if dy == 0 else far.at[(1 - dy) // 2]
        speed_copies.append(send(
            source.at[pl.ds(*src_x), pl.ds(src_y, count_y)],
            gspeed.at[gz, pl.ds(dst_x, src_x[1]), pl.ds(dst_y, count_y)],
            speed_send.at[number], recv_sem, at(dx, dy, z),
        ))

    turned = [
        pltpu.roll(strip_s[...], (NZ - 2 * D + D * gz - PITCH * (tile + 1) + NZ) % NZ, 2)
        for tile in (NY // 8 - 1, 0)
    ]
    near_all = jnp.broadcast_to(near[None], (NX, 8, NZ))
    upper = last_rows(history.at[5], history, bricks.at[1], OY + NY - 7)
    upper = jnp.where(near_all, turned[0], roll(upper, 1, 1))
    lower = last_rows(history.at[5], history, bricks.at[1], OY - 1)
    lower = jnp.where(near_all, turned[1], roll(lower, -1, 1))
    far[0, :, pl.ds(0, 2)] = upper[:, 6:8]
    far[1, :, pl.ds(0, 2)] = lower[:, 0:2]
    for dx in (0, -1, 1):
        for dy, z in ((1, 0), (-1, 1)):
            tell(dx, dy, z, len(speed_copies), speed_recv_b.at[dx + 1, gz])

    def brick_end(x, temp_before, heat):
        temp, fast = outcome([history[s, x] for s in range(1, 6)], temp_before, heat)
        for tile in range(NY // 8):
            cut = slice(OY + 8 * tile, OY + 8 * tile + 8)
            back = (NZ - 2 * D + D * gz - PITCH * (tile + 1) + NZ) % NZ
            put = pl.ds(8 * tile, 8)
            temp_own[x - D, put] = jnp.where(
                near, pltpu.roll(strip_t[x - D], back, 1), temp[cut]
            )
            speed[x - D, put] = jnp.where(
                near, pltpu.roll(strip_s[x - D], back, 1), fast[cut]
            )

    substep(history.at[5], None, bricks.at[1], 6, brick_end)
    temp_save = pltpu.make_async_copy(temp_own, temp_out, save_sem.at[0])
    temp_save.start()

    for dx in (-1, 1):
        for z in range(2):
            tell(dx, 0, z, len(speed_copies), speed_recv_a.at[dx + 1, gz])
    tell(0, 0, other, len(speed_copies), speed_recv_a.at[1, gz])
    keep = pltpu.make_async_copy(
        speed.at[:, pl.ds(14 * gz, 18)],
        gspeed.at[gz, pl.ds(2, NX), pl.ds(8 - 2 * gz, 18)],
        local_sem,
    )
    keep.start()

    for copy in lab_copies:
        copy.wait()
    row_g = rows((GY, NZ))
    outside_g = ((row_g < 8) & (gy + gz == 0)) | (
        (row_g >= 8 + GR) & (gy + gz == ngy)
    )

    def border(x):
        outside = outside_g | ((x < 2) & (gx == 0)) | ((x >= 2 + NX) & (gx == ngx - 1))
        for half in range(2):
            lab[0, half, x] = jnp.where(outside, 0, lab[0, half, x])
            lab[1, half, x] = jnp.where(outside, -1, lab[1, half, x])

    loop(0, GX, 2, border)
    wide = pl.ds(7, 24)
    own = pl.ds(8, GR)

    def first_labels(x):
        codes = [lab[1, half, x, wide] for half in range(2)]
        sides = pick(lab.at[0], x, 7, 24, codes)
        for half in range(2):
            lab1[half, x, wide] = sides[half]
            reach1[half, x, wide] = lookup(tables, sides[half], codes[half])

    loop(1, GX - 1, 3, first_labels)

    def second_labels(x):
        codes = [lab[2, half, x, own] for half in range(2)]
        sides = pick(lab1, x, 8, GR, codes)
        for half in range(2):
            grain_own[x - 2, :, pl.ds(half * NZ, NZ)] = sides[half] >> 6
            reach2[half, x, own] = lookup(tables, sides[half], codes[half])

    loop(2, GX - 2, 4, second_labels)
    grain_save = pltpu.make_async_copy(grain_own, grain_out, save_sem.at[1])
    grain_save.start()

    for copy in speed_copies:
        copy.wait_send()
    keep.wait()

    def heard(count_x, count_y, recv_sem):
        pltpu.make_async_remote_copy(
            src_ref=speed.at[pl.ds(0, count_x), pl.ds(0, count_y)],
            dst_ref=gspeed.at[0, pl.ds(0, count_x), pl.ds(0, count_y)],
            send_sem=speed_send.at[0], recv_sem=recv_sem,
            device_id=at(0, 0, other), device_id_type=MESH,
        ).wait_recv()

    for z in range(2):
        for dx in (-1, 1):
            heard(2, 18, speed_recv_a.at[dx + 1, z])
            heard(1, 1, speed_recv_b.at[dx + 1, z])
        heard(NX, 2, speed_recv_b.at[1, z])
    heard(NX, 18, speed_recv_a.at[1, other])

    def first_growth(x):
        codes = [lab[1, half, x, wide] for half in range(2)]
        sides = pick(gspeed, x, 7, 24, codes)
        for half in range(2):
            solid = lab1[half, x, wide] > 0
            caught = jnp.maximum(sides[half] - reach1[half, x, wide], 0.0)
            envelope = jnp.where(solid & (codes[half] >= 0), caught, 0.0)
            env1[half, x, wide] = envelope
            grown1[half, x, wide] = envelope + jnp.where(solid, gspeed[half, x, wide], 0.0)

    loop(1, GX - 1, 6, first_growth)

    def second_growth(x):
        codes = [lab[2, half, x, own] for half in range(2)]
        sides = pick(grown1, x, 8, GR, codes)
        for half in range(2):
            caught = jnp.maximum(sides[half] - reach2[half, x, own], 0.0)
            env_own[x - 2, :, pl.ds(half * NZ, NZ)] = jnp.where(
                codes[half] < 0, env1[half, x, own], caught
            )

    saves = [temp_save, grain_save]
    for part in range(2):
        cut = pl.ds(NX // 2 * part, NX // 2)
        loop(2 + NX // 2 * part, 2 + NX // 2 * (part + 1), 8, second_growth)
        saves.append(pltpu.make_async_copy(env_own.at[cut], env_out.at[cut], save_sem.at[2 + part]))
        saves[-1].start()
    for save in saves:
        save.wait()


def handing_on(*refs):
    sources, targets, held, sems = refs[:3], refs[3:6], refs[6:9], refs[9]
    fetches = [pltpu.make_async_copy(sources[i], held[i], sems.at[0, i]) for i in range(3)]
    stores = [pltpu.make_async_copy(held[i], targets[i], sems.at[1, i]) for i in range(3)]
    for fetch in fetches:
        fetch.start()
    for fetch, store in zip(fetches, stores):
        fetch.wait()
        store.start()
    for store in stores:
        store.wait()


def body(*args):
    hbm = pl.BlockSpec(memory_space=pltpu.HBM)
    f32, i32 = jnp.float32, jnp.int32
    dma = pltpu.SemaphoreType.DMA
    growth = (2, GX, GY, NZ)
    results = (
        jax.ShapeDtypeStruct((NX, NY, NZ), f32),
        jax.ShapeDtypeStruct((NX, GR, 2 * NZ), f32),
        jax.ShapeDtypeStruct((NX, GR, 2 * NZ), i32),
    )
    made = pl.pallas_call(
        kernel,
        out_shape=results,
        in_specs=[hbm] * 9,
        out_specs=(hbm, hbm, hbm),
        scratch_shapes=[
            pltpu.VMEM((NX, NY, NZ), f32),
            pltpu.VMEM((NX, NY, NZ), f32),
            pltpu.VMEM((NX, NY, NZ), i32),
            pltpu.VMEM((NX, GR, 2 * NZ), i32),
            pltpu.VMEM((NX, GR, 2 * NZ), i32),
            pltpu.VMEM((NX, GR, 2 * NZ), i32),
            pltpu.VMEM((2, NX, GR, 2 * NZ), i32),
            pltpu.SMEM((1, 1, 8), i32),
            pltpu.VMEM((3, 64), f32),
            dma((9,)),
            pltpu.VMEM((NX, NY, NZ), f32),
            pltpu.VMEM((NX, GR, 2 * NZ), f32),
            pltpu.VMEM((NX, GR, 2 * NZ), i32),
            dma((4,)),
            pltpu.VMEM((2, EX, EY, NZ), f32),
            pltpu.VMEM((6, EX, EY, NZ), f32),
            pltpu.VMEM((EX, 8, NZ), f32),
            pltpu.VMEM((EX, 8, NZ), f32),
            pltpu.VMEM((EX, 8, NZ), f32),
            pltpu.VMEM((EX, 8, NZ), f32),
            pltpu.VMEM((NX, NY, NZ), f32),
            pltpu.VMEM((2, NX, 8, NZ), f32),
            pltpu.VMEM((NX, 8, NZ), f32),
            pltpu.VMEM((NX, 8, NZ), f32),
            pltpu.VMEM((3,) + growth, i32),
            pltpu.VMEM(growth, i32),
            pltpu.VMEM(growth, f32),
            pltpu.VMEM(growth, f32),
            pltpu.VMEM(growth, f32),
            pltpu.VMEM(growth, f32),
            pltpu.VMEM(growth, f32),
            dma((8,)), dma((8,)), dma, dma,
            dma((14,)), dma((3, 2)), dma((3, 2)), dma, dma((8,)), dma((8,)),
        ],
        compiler_params=pltpu.CompilerParams(
            collective_id=0, has_side_effects=True, vmem_limit_bytes=62 << 20
        ),
    )(*args)
    return pl.pallas_call(
        handing_on,
        out_shape=results,
        in_specs=[hbm] * 3,
        out_specs=(hbm, hbm, hbm),
        scratch_shapes=[pltpu.VMEM(r.shape, r.dtype) for r in results] + [dma((2, 3))],
        compiler_params=pltpu.CompilerParams(vmem_limit_bytes=62 << 20),
    )(*made)


def solution(mesh):
    thermal = P("gx", "gy", "gz")
    growth = P("gx", ("gy", "gz"), None)
    placed = (
        thermal, thermal, thermal, growth, growth, growth,
        P(None, "gx", ("gy", "gz"), None), growth, P(),
    )
    return jax.shard_map(
        body, mesh=mesh, in_specs=placed, out_specs=(thermal, growth, growth), check_vma=False
    )
```
